256 devices in a mesh: ctx: 32 (over y, x, core), head: 8 (over z).
Axes of the slice: x: 4, y: 4, z: 8, core: 2. Of those that a mesh axis runs over, the one named last changes fastest.
Arguments:
- queries: bfloat16 [16384, 4096], P(('ctx', 'head')), may hold values from -6 to 6
- key_states: bfloat16 [16384, 1024], P(('ctx', 'head')), may hold values from -6 to 6
- value_states: bfloat16 [16384, 1024], P(('ctx', 'head')), may hold values from -6 to 6
- out_grad: bfloat16 [16384, 4096], P(('ctx', 'head')), may hold values from -6 to 6
- doc_lengths: int32 [13], replicated, may hold values from 1 to 3073, as said below
- key_first: int32 [64], replicated, may hold values from 0 to 57, as said below
- block_order: int32 [64], replicated, may hold values from 0 to 63, as said below
Outputs:
- attended: bfloat16 [16384, 4096], P('ctx', 'head')
- query_grad: bfloat16 [16384, 4096], P('ctx', 'head')
- key_grad: bfloat16 [16384, 1024], P('ctx', 'head')
- value_grad: bfloat16 [16384, 1024], P('ctx', 'head')
The draws below stay inside these ranges and needn't reach their ends.
Inputs may be any that keep to these rules, and one draw needn't show every extreme that they name: `doc_lengths`: they sum to 16384; the last document is the longest, of 3073 tokens. key_first[b] is the later of b - 6 and the block that holds the first token of the document holding token b * 256. `block_order`: A permutation of the 64 sequence blocks.
All inputs are finite; a program needn't handle non-finite values.
Results may differ from the reference program's by a relative error of at most 0.035.
Values may be sent and summed in bfloat16 or wider, within the bound.
A program may use at most 128 MiB of HBM per device.

```python
import jax
import jax.numpy as jnp
from jax import lax

QH = 32
KVH = 8
HD = 128
BLOCK = 256
BLK_DEV = 2
TOKENS = 16384
REACH = 6
MOST = 3073
DOC_PAIRS = 6


def document_plan(key):
    block_count = TOKENS // BLOCK
    remaining = TOKENS - MOST
    typical = remaining // (2 * DOC_PAIRS)
    leftover = remaining - typical * 2 * DOC_PAIRS
    spread = jax.random.randint(jax.random.fold_in(key, 11), (DOC_PAIRS,), 0, typical // 2 + 1)
    others = jnp.concatenate([typical + spread, typical - spread]).astype(jnp.int32)
    others = others + (jnp.arange(2 * DOC_PAIRS) < leftover).astype(jnp.int32)
    others = jax.random.permutation(jax.random.fold_in(key, 12), others)
    lengths = jnp.concatenate([others, jnp.full((1,), MOST, jnp.int32)]).astype(jnp.int32)
    doc_ends = jnp.cumsum(lengths)
    doc_starts = doc_ends - lengths
    block_ids = jnp.arange(block_count, dtype=jnp.int32)
    first_tokens = block_ids * BLOCK
    holding = jnp.max(jnp.where(doc_starts[None, :] <= first_tokens[:, None], doc_starts[None, :], 0), axis=1)
    key_first = jnp.maximum(holding // BLOCK, block_ids - REACH).astype(jnp.int32)
    workload = block_ids - key_first + 1
    ranked = jnp.argsort(-(workload * block_count + block_ids)).astype(jnp.int32)
    device_count = block_count // BLK_DEV
    rank_ids = jnp.arange(block_count, dtype=jnp.int32)
    rounds = rank_ids // device_count
    within = rank_ids % device_count
    device = jnp.where(rounds % 2 == 0, within, device_count - 1 - within)
    shuffle = jax.random.permutation(jax.random.fold_in(key, 13), device_count).astype(jnp.int32)
    position = shuffle[device] * BLK_DEV + rounds
    placed = jnp.zeros((block_count,), jnp.int32).at[position].set(ranked)
    return (lengths, key_first, placed)


def draw_doc_lengths(key, part):
    shared = document_plan(key)
    return shared[0]


def draw_key_first(key, part):
    shared = document_plan(key)
    return shared[1]


def draw_block_order(key, part):
    shared = document_plan(key)
    return shared[2]


def draw_queries(key, part):
    key = jax.random.fold_in(key, 4)
    values = jnp.clip(jax.random.normal(key, (TOKENS, QH * HD)), -6.0, 6.0)
    return values.astype(jnp.bfloat16)


def draw_key_states(key, part):
    key = jax.random.fold_in(key, 5)
    values = jnp.clip(jax.random.normal(key, (TOKENS, KVH * HD)), -6.0, 6.0)
    return values.astype(jnp.bfloat16)


def shard_levels(rng, extent, cuts, least, top_value):
    gain = 1.0
    for dim, parts in cuts:
        steps = jax.random.uniform(jax.random.fold_in(jax.random.fold_in(rng, 6), dim), (parts,), jnp.float32, least / len(cuts), top_value / len(cuts))
        gain = gain * jnp.repeat(jnp.exp(steps), extent[dim] // parts).reshape((-1,) + (1,) * (len(extent) - 1 - dim))
    return gain


def centred(stream_key, dims, width, bound, split=(), kind=jnp.bfloat16):
    result = jax.random.normal(stream_key, dims, jnp.float32) * width
    if len(split) > 0:
        result = shard_levels(stream_key, dims, split, -0.22, 0.18) * result
    return jnp.clip(result, min=-bound, max=bound).astype(kind)


def setup_inputs(seed: int = 0) -> dict:
    key_of = jax.random.split(jax.random.key(seed), 8)
    queries = draw_queries(jax.random.fold_in(key_of[7], 71), 0)
    key_states = draw_key_states(jax.random.fold_in(key_of[7], 71), 0)
    value_states = centred(key_of[2], (TOKENS, KVH * HD), 1.0, 6.0, ((0, 256),))
    out_grad = centred(key_of[3], (TOKENS, QH * HD), 1.0, 6.0, ((0, 256),))
    doc_lengths = draw_doc_lengths(jax.random.fold_in(key_of[7], 71), 0)
    key_first = draw_key_first(jax.random.fold_in(key_of[7], 71), 0)
    block_order = draw_block_order(jax.random.fold_in(key_of[7], 71), 0)
    return {"queries": queries, "key_states": key_states, "value_states": value_states, "out_grad": out_grad, "doc_lengths": doc_lengths, "key_first": key_first, "block_order": block_order}


def document_ids(positions, doc_lengths):
    doc_ends = jnp.cumsum(doc_lengths).astype(jnp.int32)
    return jnp.sum((positions[:, None] >= doc_ends[None, :]).astype(jnp.int32), axis=1)


def reference(queries, key_states, value_states, out_grad, doc_lengths, key_first, block_order):
    block_count = TOKENS // BLOCK
    group_size = QH // KVH
    score_scale = HD ** -0.5
    window = min((REACH + 1) * BLOCK, TOKENS)
    inverse = jnp.zeros((block_count,), jnp.int32).at[block_order].set(jnp.arange(block_count, dtype=jnp.int32))

    def to_sequence(array):
        return array.reshape(block_count, BLOCK, array.shape[1])[inverse].reshape(TOKENS, array.shape[1])

    def to_layout(array):
        return array.reshape(block_count, BLOCK, array.shape[1])[block_order].reshape(TOKENS, array.shape[1])

    seq_queries = to_sequence(queries)
    seq_keys = to_sequence(key_states)
    seq_values = to_sequence(value_states)
    seq_grads = to_sequence(out_grad)
    positions = jnp.arange(TOKENS, dtype=jnp.int32)
    documents = document_ids(positions, doc_lengths)

    def one_block(running, query_block):
        key_sum, value_sum = running
        query_start = query_block * BLOCK
        key_start = jnp.maximum(query_start + BLOCK - window, 0)
        block_queries = lax.dynamic_slice_in_dim(seq_queries, query_start, BLOCK, 0).astype(jnp.float32).reshape(BLOCK, KVH, group_size, HD)
        block_grads = lax.dynamic_slice_in_dim(seq_grads, query_start, BLOCK, 0).astype(jnp.float32).reshape(BLOCK, KVH, group_size, HD)
        window_keys = lax.dynamic_slice_in_dim(seq_keys, key_start, window, 0).astype(jnp.float32).reshape(window, KVH, HD)
        window_values = lax.dynamic_slice_in_dim(seq_values, key_start, window, 0).astype(jnp.float32).reshape(window, KVH, HD)
        query_pos = query_start + jnp.arange(BLOCK, dtype=jnp.int32)
        key_pos = key_start + jnp.arange(window, dtype=jnp.int32)
        query_docs = lax.dynamic_slice_in_dim(documents, query_start, BLOCK, 0)
        key_docs = lax.dynamic_slice_in_dim(documents, key_start, window, 0)
        allowed = (query_docs[:, None] == key_docs[None, :]) & (key_pos[None, :] <= query_pos[:, None]) & (key_pos[None, :] // BLOCK >= key_first[query_block])
        scores = jnp.einsum("qhgd,khd->hgqk", block_queries, window_keys) * score_scale
        scores = jnp.where(allowed, scores, -jnp.inf)
        maxima = jnp.max(scores, axis=-1, keepdims=True)
        log_total = maxima + jnp.log(jnp.sum(jnp.exp(scores - maxima), axis=-1, keepdims=True))
        probs = jnp.exp(scores - log_total)
        weights = lax.optimization_barrier(probs.astype(jnp.bfloat16)).astype(jnp.float32)
        attended = lax.optimization_barrier(jnp.einsum("hgqk,khd->qhgd", weights, window_values).astype(jnp.bfloat16))
        delta = jnp.einsum("qhgd,qhgd->hgq", block_grads, attended.astype(jnp.float32))
        prob_grad = jnp.einsum("qhgd,khd->hgqk", block_grads, window_values)
        score_grad = lax.optimization_barrier((probs * (prob_grad - delta[..., None])).astype(jnp.bfloat16)).astype(jnp.float32)
        query_grad = (jnp.einsum("hgqk,khd->qhgd", score_grad, window_keys) * score_scale).astype(jnp.bfloat16)
        key_part = jnp.einsum("hgqk,qhgd->khd", score_grad, block_queries) * score_scale
        value_part = jnp.einsum("hgqk,qhgd->khd", weights, block_grads)
        key_sum = lax.dynamic_update_slice_in_dim(key_sum, lax.dynamic_slice_in_dim(key_sum, key_start, window, 0) + key_part, key_start, 0)
        value_sum = lax.dynamic_update_slice_in_dim(value_sum, lax.dynamic_slice_in_dim(value_sum, key_start, window, 0) + value_part, key_start, 0)
        return (key_sum, value_sum), (attended.reshape(BLOCK, QH * HD), query_grad.reshape(BLOCK, QH * HD))

    start_sums = (jnp.zeros((TOKENS, KVH, HD), jnp.float32), jnp.zeros((TOKENS, KVH, HD), jnp.float32))
    (key_sum, value_sum), (attended_blocks, grad_blocks) = lax.scan(one_block, start_sums, jnp.arange(block_count, dtype=jnp.int32))
    attended = to_layout(attended_blocks.reshape(TOKENS, QH * HD))
    query_grad = to_layout(grad_blocks.reshape(TOKENS, QH * HD))
    key_grad = to_layout(key_sum.reshape(TOKENS, KVH * HD).astype(jnp.bfloat16))
    value_grad = to_layout(value_sum.reshape(TOKENS, KVH * HD).astype(jnp.bfloat16))
    return attended, query_grad, key_grad, value_grad
```

```python
import functools

import jax
import jax.numpy as jnp
from jax import lax
from jax.experimental import pallas as pl
from jax.experimental.pallas import tpu as pltpu
from jax.sharding import PartitionSpec as P

HD = 128
BLOCK = 256
SPAN = 7
MESH = pl.DeviceIdType.MESH
LOG2E = 1.4426950408889634


def greet(ctx_count, head_count, ctx_me, head_me, with_heads):
    barrier = pltpu.get_barrier_semaphore()

    def greet_ctx(r, carry):
        pl.semaphore_signal(
            barrier, inc=1, device_id=(lax.rem(ctx_me + r, ctx_count), head_me), device_id_type=MESH
        )
        return carry

    lax.fori_loop(1, ctx_count, greet_ctx, 0)
    total = ctx_count - 1
    if with_heads:

        def greet_head(r, carry):
            pl.semaphore_signal(
                barrier,
                inc=1,
                device_id=(ctx_me, lax.rem(head_me + r, head_count)),
                device_id_type=MESH,
            )
            return carry

        lax.fori_loop(1, head_count, greet_head, 0)
        total += head_count - 1
    pl.semaphore_wait(barrier, total)


def drain(ref, sem):
    pltpu.make_async_copy(ref, ref, sem).wait()


def spread_kernel(
    ctx_count,
    head_count,
    slots,
    list_ref,
    q_ref,
    k_ref,
    v_ref,
    g_ref,
    q_out,
    g_out,
    kv_out,
    landed,
    pieces,
    staged,
    kv_send,
    kv_recv,
    wide_send,
    wide_recv,
    piece_send,
    piece_recv,
    list_send,
    list_recv,
):
    ctx_me = lax.axis_index("ctx")
    head_me = lax.axis_index("head")
    rows = k_ref.shape[0]
    wide = q_ref.shape[1] // head_count
    part_rows = pieces.shape[1]
    greet(ctx_count, head_count, ctx_me, head_me, True)

    my_rows = pl.ds(pl.multiple_of(head_me * rows, rows), rows)
    for which, ref in enumerate((k_ref, v_ref)):

        def send_narrow(r, carry, which=which, ref=ref):
            peer = lax.rem(head_me + r, head_count)
            pltpu.make_async_remote_copy(
                src_ref=ref.at[:, pl.ds(pl.multiple_of(peer * HD, HD), HD)],
                dst_ref=landed.at[which, my_rows],
                send_sem=kv_send,
                recv_sem=kv_recv,
                device_id=(ctx_me, peer),
                device_id_type=MESH,
            ).start()
            return carry

        lax.fori_loop(1, head_count, send_narrow, 0)
        pltpu.make_async_copy(
            ref.at[:, pl.ds(pl.multiple_of(head_me * HD, HD), HD)],
            landed.at[which, my_rows],
            kv_recv,
        ).start()
    for which, (ref, out) in enumerate(((q_ref, q_out), (g_ref, g_out))):

        def send_wide(r, carry, ref=ref, out=out, which=which):
            peer = lax.rem(head_me + r, head_count)
            pltpu.make_async_remote_copy(
                src_ref=ref.at[:, pl.ds(pl.multiple_of(peer * wide, wide), wide)],
                dst_ref=out.at[my_rows],
                send_sem=wide_send.at[which],
                recv_sem=wide_recv.at[which],
                device_id=(ctx_me, peer),
                device_id_type=MESH,
            ).start()
            return carry

        lax.fori_loop(1, head_count, send_wide, 0)
        pltpu.make_async_copy(
            ref.at[:, pl.ds(pl.multiple_of(head_me * wide, wide), wide)],
            out.at[my_rows],
            wide_recv.at[which],
        ).start()

    drain(landed, kv_recv)
    blocks = landed.shape[1] // BLOCK
    my_blocks = pl.ds(ctx_me * blocks, blocks)
    my_kind = lax.rem(ctx_me, 2)
    my_part = lax.div(ctx_me, 2)

    def piece_of(device, block):
        start = pl.multiple_of(block * BLOCK + lax.div(device, 2) * part_rows, part_rows)
        return landed.at[lax.rem(device, 2), pl.ds(start, part_rows)]

    for block in range(blocks):

        def send_piece(r, carry, block=block):
            peer = lax.rem(ctx_me + r, ctx_count)
            pltpu.make_async_remote_copy(
                src_ref=piece_of(peer, block),
                dst_ref=pieces.at[ctx_me * blocks + block],
                send_sem=piece_send,
                recv_sem=piece_recv,
                device_id=(peer, head_me),
                device_id_type=MESH,
            ).start()
            return carry

        lax.fori_loop(1, ctx_count, send_piece, 0)
        pltpu.make_async_copy(
            piece_of(ctx_me, block), pieces.at[ctx_me * blocks + block], piece_recv
        ).start()
    drain(pieces, piece_recv)

    my_part_rows = pl.ds(pl.multiple_of(my_part * part_rows, part_rows), part_rows)

    def stage(peer):
        for slot in range(slots):
            staged[peer, slot] = pieces[list_ref[peer * slots + slot]]

    def send_listed(r, carry):
        peer = lax.rem(ctx_me + r, ctx_count)
        stage(peer)
        pltpu.make_async_remote_copy(
            src_ref=staged.at[peer],
            dst_ref=kv_out.at[my_kind, :, my_part_rows],
            send_sem=list_send,
            recv_sem=list_recv,
            device_id=(peer, head_me),
            device_id_type=MESH,
        ).start()
        return carry

    lax.fori_loop(1, ctx_count, send_listed, 0)
    stage(ctx_me)
    pltpu.make_async_copy(
        staged.at[ctx_me], kv_out.at[my_kind, :, my_part_rows], list_recv
    ).start()

    drain(kv_out, list_recv)
    drain(q_out, wide_recv.at[0])
    drain(g_out, wide_recv.at[1])
    sent = rows * (head_count - 1)
    drain(landed.at[0, pl.ds(0, sent)], kv_send)
    drain(landed.at[1, pl.ds(0, sent)], kv_send)
    drain(q_out.at[pl.ds(0, sent)], wide_send.at[0])
    drain(g_out.at[pl.ds(0, sent)], wide_send.at[1])
    drain(pieces.at[pl.ds(0, (ctx_count - 1) * blocks)], piece_send)
    drain(staged.at[pl.ds(0, ctx_count - 1)], list_send)


def gather_kernel(
    ctx_count,
    slots,
    table_ref,
    part_ref,
    out_ref,
    arrived,
    summed,
    part_send,
    part_recv,
    sum_send,
    sum_recv,
):
    ctx_me = lax.axis_index("ctx")
    head_me = lax.axis_index("head")
    part_rows = arrived.shape[1]
    blocks = summed.shape[1]
    greet(ctx_count, 1, ctx_me, head_me, False)
    my_slots = pl.ds(ctx_me * slots, slots)

    def rows_of(device):
        return pl.ds(pl.multiple_of(lax.div(device, 2) * part_rows, part_rows), part_rows)

    def send_part(r, carry):
        peer = lax.rem(ctx_me + r, ctx_count)
        pltpu.make_async_remote_copy(
            src_ref=part_ref.at[lax.rem(peer, 2), :, rows_of(peer)],
            dst_ref=arrived.at[my_slots],
            send_sem=part_send,
            recv_sem=part_recv,
            device_id=(peer, head_me),
            device_id_type=MESH,
        ).start()
        return carry

    lax.fori_loop(1, ctx_count, send_part, 0)
    pltpu.make_async_copy(
        part_ref.at[lax.rem(ctx_me, 2), :, rows_of(ctx_me)], arrived.at[my_slots], part_recv
    ).start()
    arrived[ctx_count * slots] = jnp.zeros(arrived.shape[1:], arrived.dtype)
    every = arrived.at[pl.ds(0, ctx_count * slots)]
    drain(every, part_recv)

    def add_up(peer):
        for block in range(blocks):
            first = (peer * blocks + block) * SPAN
            total = arrived[table_ref[first]].astype(jnp.float32)
            for step in range(1, SPAN):
                total = total + arrived[table_ref[first + step]].astype(jnp.float32)
            summed[peer, block] = total.astype(summed.dtype)

    def send_sum(r, carry):
        peer = lax.rem(ctx_me + r, ctx_count)
        add_up(peer)
        pltpu.make_async_remote_copy(
            src_ref=summed.at[peer],
            dst_ref=out_ref.at[lax.rem(ctx_me, 2), :, rows_of(ctx_me)],
            send_sem=sum_send,
            recv_sem=sum_recv,
            device_id=(peer, head_me),
            device_id_type=MESH,
        ).start()
        return carry

    lax.fori_loop(1, ctx_count, send_sum, 0)
    add_up(ctx_me)
    pltpu.make_async_copy(
        summed.at[ctx_me], out_ref.at[lax.rem(ctx_me, 2), :, rows_of(ctx_me)], sum_recv
    ).start()
    drain(out_ref, sum_recv)
    drain(arrived.at[pl.ds(0, (ctx_count - 1) * slots)], part_send)
    drain(summed.at[pl.ds(0, ctx_count - 1)], sum_send)


def attend_kernel(
    docs,
    group,
    meta_ref,
    q_ref,
    g_ref,
    kv_ref,
    o_ref,
    dq_ref,
    part_ref,
    scores,
    offset,
    maxima,
    totals,
    running,
    delta,
):
    scale = HD**-0.5
    exp_scale = scale * LOG2E
    rows_last = lax.broadcasted_iota(jnp.int32, (BLOCK, BLOCK), 0)
    cols_last = lax.broadcasted_iota(jnp.int32, (BLOCK, BLOCK), 1)
    contract_last = (((1,), (1,)), ((), ()))
    contract_first = (((0,), (0,)), ((), ()))

    def twice(ref):
        half = ref[...]
        return jnp.concatenate([half, half], axis=1)

    def query_block(index, carry):
        block = meta_ref[index]
        count = meta_ref[2 + index]
        base = index * meta_ref[2]
        rows = pl.ds(pl.multiple_of(index * BLOCK, BLOCK), BLOCK)
        q_pos = rows_last + block * BLOCK
        first = jnp.zeros((BLOCK, BLOCK), jnp.int32)
        for doc in range(docs - 1):
            end = meta_ref[4 + doc]
            first = jnp.where(q_pos >= end, end, first)
        offset[...] = cols_last - first
        maxima[...] = jnp.full_like(maxima, -jnp.inf)
        totals[...] = jnp.zeros_like(totals)
        running[...] = jnp.zeros_like(running)

        def score_step(turn, carry):
            keys = kv_ref[0, base + turn]
            allowed = (offset[...] >= (turn - block) * BLOCK) & (
                cols_last - rows_last <= turn * BLOCK
            )
            bias = jnp.where(allowed, 0.0, -jnp.inf)
            for g in range(group):
                tile = lax.dot_general(
                    q_ref[rows, g * HD : (g + 1) * HD],
                    keys,
                    contract_last,
                    preferred_element_type=jnp.float32,
                )
                tile = tile + bias
                scores[turn, g] = tile
                maxima[g] = jnp.maximum(
                    maxima[g], jnp.maximum(tile[:, :HD], tile[:, HD:])
                )
            return carry

        lax.fori_loop(0, count, score_step, 0)
        for g in range(group):
            top = jnp.max(maxima[g], axis=1, keepdims=True) * exp_scale
            maxima[g] = jnp.broadcast_to(top, (BLOCK, HD))

        def weight_step(turn, carry):
            values = kv_ref[1, base + turn]
            for g in range(group):
                tile = jnp.exp2(scores[turn, g] * exp_scale - twice(maxima.at[g]))
                scores[turn, g] = tile
                totals[g] = totals[g] + (tile[:, :HD] + tile[:, HD:])
                running[g] = running[g] + jnp.dot(
                    tile.astype(jnp.bfloat16), values, preferred_element_type=jnp.float32
                )
            return carry

        lax.fori_loop(0, count, weight_step, 0)
        for g in range(group):
            columns = slice(g * HD, (g + 1) * HD)
            inverse = 1.0 / jnp.sum(totals[g], axis=1, keepdims=True)
            totals[g] = jnp.broadcast_to(inverse, (BLOCK, HD))
            result = (running[g] * totals[g]).astype(jnp.bfloat16)
            o_ref[rows, columns] = result
            product = result.astype(jnp.float32) * g_ref[rows, columns].astype(jnp.float32)
            delta[g] = jnp.broadcast_to(
                jnp.sum(product, axis=1, keepdims=True), (BLOCK, HD)
            )
        running[...] = jnp.zeros_like(running)

        def grad_step(turn, carry):
            keys = kv_ref[0, base + turn]
            values = kv_ref[1, base + turn]
            key_grad = jnp.zeros((BLOCK, HD), jnp.float32)
            value_grad = jnp.zeros((BLOCK, HD), jnp.float32)
            for g in range(group):
                columns = slice(g * HD, (g + 1) * HD)
                out_grad = g_ref[rows, columns]
                weights = scores[turn, g] * twice(totals.at[g])
                prob_grad = lax.dot_general(
                    out_grad, values, contract_last, preferred_element_type=jnp.float32
                )
                score_grad = (weights * (prob_grad - twice(delta.at[g]))).astype(jnp.bfloat16)
                running[g] = running[g] + jnp.dot(
                    score_grad, keys, preferred_element_type=jnp.float32
                )
                key_grad = key_grad + lax.dot_general(
                    score_grad,
                    q_ref[rows, columns],
                    contract_first,
                    preferred_element_type=jnp.float32,
                )
                value_grad = value_grad + lax.dot_general(
                    weights.astype(jnp.bfloat16),
                    out_grad,
                    contract_first,
                    preferred_element_type=jnp.float32,
                )
            part_ref[0, base + turn] = (key_grad * scale).astype(jnp.bfloat16)
            part_ref[1, base + turn] = value_grad.astype(jnp.bfloat16)
            return carry

        lax.fori_loop(0, count, grad_step, 0)
        for g in range(group):
            dq_ref[rows, g * HD : (g + 1) * HD] = (running[g] * scale).astype(jnp.bfloat16)
        return carry

    lax.fori_loop(0, 2, query_block, 0)


def spread(slots, ids, ctx_count, head_count, listing, queries, keys, values, grads):
    rows = queries.shape[0] * head_count
    wide = queries.shape[1] // head_count
    blocks = rows // BLOCK
    part_rows = 2 * BLOCK // ctx_count
    anywhere = pl.BlockSpec(memory_space=pl.ANY)
    bf16 = jnp.bfloat16
    return pl.pallas_call(
        functools.partial(spread_kernel, ctx_count, head_count, slots),
        out_shape=(
            jax.ShapeDtypeStruct((rows, wide), bf16),
            jax.ShapeDtypeStruct((rows, wide), bf16),
            jax.ShapeDtypeStruct((2, slots, BLOCK, HD), bf16),
        ),
        in_specs=[pl.BlockSpec(memory_space=pltpu.SMEM)] + [anywhere] * 4,
        out_specs=[anywhere] * 3,
        scratch_shapes=[
            pltpu.VMEM((2, rows, HD), bf16),
            pltpu.VMEM((ctx_count * blocks, part_rows, HD), bf16),
            pltpu.VMEM((ctx_count, slots, part_rows, HD), bf16),
            pltpu.SemaphoreType.DMA,
            pltpu.SemaphoreType.DMA,
            pltpu.SemaphoreType.DMA((2,)),
            pltpu.SemaphoreType.DMA((2,)),
            pltpu.SemaphoreType.DMA,
            pltpu.SemaphoreType.DMA,
            pltpu.SemaphoreType.DMA,
            pltpu.SemaphoreType.DMA,
        ],
        compiler_params=pltpu.CompilerParams(
            collective_id=ids, has_side_effects=True, vmem_limit_bytes=48 << 20
        ),
        name="spread",
    )(listing, queries, keys, values, grads)


def attend(slots, docs, meta, queries, grads, kv):
    rows, wide = queries.shape
    group = wide // HD
    whole = pl.BlockSpec(memory_space=pltpu.VMEM)
    stat = pltpu.VMEM((group, BLOCK, HD), jnp.float32)
    return pl.pallas_call(
        functools.partial(attend_kernel, docs, group),
        out_shape=(
            jax.ShapeDtypeStruct((rows, wide), jnp.bfloat16),
            jax.ShapeDtypeStruct((rows, wide), jnp.bfloat16),
            jax.ShapeDtypeStruct(kv.shape, jnp.bfloat16),
        ),
        in_specs=[pl.BlockSpec(memory_space=pltpu.SMEM)] + [whole] * 3,
        out_specs=[whole] * 3,
        scratch_shapes=[
            pltpu.VMEM((SPAN, group, BLOCK, BLOCK), jnp.float32),
            pltpu.VMEM((BLOCK, BLOCK), jnp.int32),
            stat,
            stat,
            stat,
            stat,
        ],
        compiler_params=pltpu.CompilerParams(vmem_limit_bytes=48 << 20),
        name="attend",
    )(meta, queries, grads, kv)


def gather(slots, ids, ctx_count, table, part):
    blocks = 2
    part_rows = 2 * BLOCK // ctx_count
    anywhere = pl.BlockSpec(memory_space=pl.ANY)
    bf16 = jnp.bfloat16
    return pl.pallas_call(
        functools.partial(gather_kernel, ctx_count, slots),
        out_shape=jax.ShapeDtypeStruct((2, blocks, BLOCK, HD), bf16),
        in_specs=[pl.BlockSpec(memory_space=pltpu.SMEM), anywhere],
        out_specs=anywhere,
        scratch_shapes=[
            pltpu.VMEM((ctx_count * slots + 1, part_rows, HD), bf16),
            pltpu.VMEM((ctx_count, blocks, part_rows, HD), bf16),
            pltpu.SemaphoreType.DMA,
            pltpu.SemaphoreType.DMA,
            pltpu.SemaphoreType.DMA,
            pltpu.SemaphoreType.DMA,
        ],
        compiler_params=pltpu.CompilerParams(
            collective_id=ids, has_side_effects=True, vmem_limit_bytes=48 << 20
        ),
        name="gather",
    )(table, part)


def on_device(ctx_count, head_count, queries, keys, values, grads, lengths, key_first, order):
    block_count = order.shape[0]
    docs = lengths.shape[0]
    ids = jnp.arange(block_count, dtype=jnp.int32)
    match = order[None, :] == ids[:, None]
    inverse = jnp.sum(jnp.where(match, ids[None, :], 0), axis=1)
    first = jnp.sum(jnp.where(match, key_first[:, None], 0), axis=0)
    counts = order - first + 1
    pair_order = order.reshape(ctx_count, 2)
    pair_counts = counts.reshape(ctx_count, 2)
    most = jnp.max(jnp.sum(pair_counts, axis=1))
    ctx_me = lax.axis_index("ctx")
    meta = jnp.concatenate(
        [
            lax.dynamic_index_in_dim(pair_order, ctx_me, 0, False),
            lax.dynamic_index_in_dim(pair_counts, ctx_me, 0, False),
            jnp.cumsum(lengths),
        ]
    )

    def branch(slots, base_id, queries, keys, values, grads):
        turn = jnp.arange(slots, dtype=jnp.int32)[None, :]
        head = pair_counts[:, :1]
        wanted = jnp.where(turn < head, pair_order[:, :1] - turn, pair_order[:, 1:] - turn + head)
        listing = jnp.sum(
            jnp.where(wanted[:, :, None] == order[None, None, :], ids[None, None, :], 0), axis=2
        ).reshape(-1)
        ahead = jnp.arange(SPAN, dtype=jnp.int32)[None, :]
        reader = order[:, None] + ahead
        seen = (reader[:, :, None] == order[None, None, :]) & (
            first[None, None, :] <= order[:, None, None]
        )
        place = (ids // 2) * slots + jnp.where(
            ids % 2 == 1, jnp.repeat(pair_counts[:, 0], 2), 0
        )
        table = jnp.sum(
            jnp.where(seen, place[None, None, :] + ahead[:, :, None] - ctx_count * slots, 0), axis=2
        ) + ctx_count * slots
        my_q, my_g, kv = spread(
            slots, base_id, ctx_count, head_count, listing, queries, keys, values, grads
        )
        attended, query_grad, part = attend(slots, docs, meta, my_q, my_g, kv)
        total = gather(slots, base_id + 1, ctx_count, table.reshape(-1), part)
        rows = attended.shape[0]
        return attended, query_grad, total[0].reshape(rows, HD), total[1].reshape(rows, HD)

    return lax.cond(
        most <= 9,
        functools.partial(branch, 9, 0),
        functools.partial(branch, 2 * SPAN, 2),
        queries,
        keys,
        values,
        grads,
    )


def solution(mesh):
    return jax.shard_map(
        functools.partial(on_device, mesh.shape["ctx"], mesh.shape["head"]),
        mesh=mesh,
        in_specs=(
            P(("ctx", "head"), None),
            P(("ctx", "head"), None),
            P(("ctx", "head"), None),
            P(("ctx", "head"), None),
            P(),
            P(),
            P(),
        ),
        out_specs=(P("ctx", "head"), P("ctx", "head"), P("ctx", "head"), P("ctx", "head")),
        check_vma=False,
    )
```

```python
import functools

import jax
import jax.numpy as jnp
from jax import lax
from jax.experimental import pallas as pl
from jax.experimental.pallas import tpu as pltpu
from jax.sharding import PartitionSpec as P

HD = 128
BLOCK = 256
SPAN = 7
CTX = 32
HEADS = 8
GROUP = 4
ROWS = 64
PIECE = 16
MESH = pl.DeviceIdType.MESH
LOG2E = 1.4426950408889634
SCALE = HD**-0.5
LAST = (((1,), (1,)), ((), ()))
FIRST = (((0,), (0,)), ((), ()))


def drain(ref, sem):
    pltpu.make_async_copy(ref, ref, sem).wait()


def loop(count, body):
    def step(index, carry):
        body(index)
        return carry

    lax.fori_loop(0, count, step, 0)


def greet(me, head):
    barrier = pltpu.get_barrier_semaphore()
    chip = lax.div(me, 2)

    def signal(ctx, z):
        pl.semaphore_signal(barrier, inc=1, device_id=(ctx, z), device_id_type=MESH)

    loop(CTX - 1, lambda r: signal(lax.rem(me + r + 1, CTX), head))
    loop(HEADS - 1, lambda r: signal(me, lax.rem(head + r + 1, HEADS)))
    for half in range(2):
        source = half * 4 + lax.div(chip, 4)
        loop(CTX - 1, lambda r: signal(lax.rem(me + r + 1, CTX), source))

        @pl.when(source != head)
        def _():
            signal(me, source)

    apart = lax.rem(lax.div(chip, 4) + 4 - lax.rem(head, 4), 4)
    pl.semaphore_wait(barrier, CTX - 1 + HEADS - 1 + 2 * CTX - 1 + lax.div(apart + 3, 4))


def fused_kernel(
    slots,
    docs,
    order_ref,
    inverse_ref,
    first_ref,
    lengths_ref,
    q_ref,
    k_ref,
    v_ref,
    g_ref,
    o_ref,
    dq_ref,
    dk_ref,
    dv_ref,
    table,
    q_buf,
    g_buf,
    g_scaled,
    q_now,
    kv,
    pieces,
    staged,
    bias,
    scores,
    probs,
    grads,
    wide_keys,
    wide_values,
    maxima,
    totals,
    delta,
    sums,
    part,
    o_buf,
    dq_buf,
    arrived,
    summed,
    piece_send,
    piece_recv,
    wide_send,
    wide_recv,
    list_send,
    list_recv,
    out_sem,
    part_send,
    part_recv,
    sum_send,
    sum_recv,
):
    me = lax.axis_index("ctx")
    head = lax.axis_index("head")
    chip, kind = lax.div(me, 2), lax.rem(me, 2)
    greet(me, head)

    def remote(src, dst, send, recv, ctx, z):
        pltpu.make_async_remote_copy(
            src_ref=src,
            dst_ref=dst,
            send_sem=send,
            recv_sem=recv,
            device_id=(ctx, z),
            device_id_type=MESH,
        ).start()

    pair = lax.div(head, 4)
    for which, ref in enumerate((k_ref, v_ref)):
        for p in range(4):
            target = (lax.rem(head, 4) * 4 + p) * 2 + which
            slot = pieces.at[me * 2 + pair]

            def send_piece(r, ref=ref, p=p, target=target, slot=slot):
                z = lax.rem(head + r, HEADS)
                src = ref.at[pl.ds(p * PIECE, PIECE), pl.ds(pl.multiple_of(z * HD, HD), HD)]
                remote(src, slot, piece_send, piece_recv, target, z)

            loop(HEADS - 1, lambda r, f=send_piece: f(r + 1))

            @pl.when(target != me)
            def _(f=send_piece):
                f(0)

            @pl.when(target == me)
            def _(ref=ref, p=p, slot=slot):
                src = ref.at[pl.ds(p * PIECE, PIECE), pl.ds(pl.multiple_of(head * HD, HD), HD)]
                pltpu.make_async_copy(src, slot, piece_recv).start()

    my_rows = pl.ds(pl.multiple_of(lax.rem(head, 4) * ROWS, ROWS), ROWS)

    def columns(z, g):
        return pl.ds(pl.multiple_of(z * GROUP * HD + g * HD, HD), HD)

    def send_heads(which, ref, buf):
        for g in range(GROUP):

            def send_wide(r, g=g):
                z = lax.rem(head + r + 1, HEADS)
                remote(
                    ref.at[:, columns(z, g)],
                    buf.at[g, pair, my_rows],
                    wide_send.at[which],
                    wide_recv.at[which, g],
                    me,
                    z,
                )

            loop(HEADS - 1, send_wide)
            pltpu.make_async_copy(
                ref.at[:, columns(head, g)], buf.at[g, pair, my_rows], wide_recv.at[which, g]
            ).start()

    send_heads(0, q_ref, q_buf)
    send_heads(1, g_ref, g_buf)

    rows = lax.broadcasted_iota(jnp.int32, (BLOCK, BLOCK), 0)
    cols = lax.broadcasted_iota(jnp.int32, (BLOCK, BLOCK), 1)

    def pair_of(device):
        block_a, block_b = order_ref[2 * device], order_ref[2 * device + 1]
        return block_a, block_b, block_a - first_ref[block_a] + 1

    block_a, block_b, count_a = pair_of(me)
    count_b = block_b - first_ref[block_b] + 1

    def chosen(t):
        return (t >= count_a).astype(jnp.int32)

    def make_bias(t):
        late = t >= count_a
        block = jnp.where(late, block_b, block_a)
        back = jnp.where(late, t - count_a, t)
        reach = jnp.where(t < count_a + count_b, back * BLOCK, -2 * BLOCK)
        low = jnp.zeros((BLOCK, BLOCK), jnp.int32)
        end = 0
        for doc in range(docs - 1):
            end = end + lengths_ref[doc]
            low = jnp.where(rows + block * BLOCK >= end, end, low)
        allowed = (cols + (block - back) * BLOCK >= low) & (cols - rows <= reach)
        bias[t] = jnp.where(allowed, 0.0, -jnp.inf)

    def rows_of(device):
        return pl.ds(pl.multiple_of(lax.div(device, 2) * PIECE, PIECE), PIECE)

    def send_lists():
        def stage(peer):
            first_block, second_block, first_count = pair_of(peer)
            for slot in range(slots):
                wanted = jnp.where(
                    slot < first_count, first_block - slot, second_block - slot + first_count
                )
                staged[peer, slot] = pieces[inverse_ref[jnp.maximum(wanted, 0)]]

        def send_list(r):
            peer = lax.rem(me + r + 1, CTX)
            stage(peer)
            remote(
                staged.at[peer],
                kv.at[kind, :, rows_of(me)],
                list_send,
                list_recv.at[kind],
                peer,
                head,
            )

        loop(CTX - 1, send_list)
        stage(me)
        pltpu.make_async_copy(
            staged.at[me], kv.at[kind, :, rows_of(me)], list_recv.at[kind]
        ).start()

    drain(pieces, piece_recv)
    pl.when(kind == 0)(send_lists)
    loop(slots, make_bias)
    drain(kv.at[0], list_recv.at[0])
    pl.when(kind == 1)(send_lists)

    def flags(t):
        late = (t >= count_a).astype(jnp.float32)
        return 1.0 - late, late

    def widen(wide, which, t):
        at = pl.ds(pl.multiple_of(t * BLOCK, BLOCK), BLOCK)
        zeros = jnp.zeros((BLOCK, HD), jnp.bfloat16)
        for i, flag in enumerate((t < count_a, t >= count_a)):
            spot = slice(i * HD, (i + 1) * HD)
            wide[at, spot] = jnp.where(flag, kv[which, t], zeros)

    unroll = 3 if slots % 3 == 0 else 2

    def tiles(body):
        def several(index):
            for u in range(unroll):
                body(index * unroll + u)

        loop(slots // unroll, several)

    def twice(half):
        return jnp.concatenate([half, half], axis=1)

    def tile_cols(t):
        return pl.ds(pl.multiple_of(t * BLOCK, BLOCK), BLOCK)

    def send_out(buf, ref, g, which):
        for i in range(2):
            pltpu.make_async_copy(
                buf.at[g, i],
                ref.at[pl.ds(i * BLOCK, BLOCK), pl.ds(pl.multiple_of(g * HD, HD), HD)],
                out_sem.at[which],
            ).start()

    def forward(g):
        drain(q_buf.at[g], wide_recv.at[0, g])
        q_now[...] = q_buf[g]
        maxima[...] = jnp.full_like(maxima, -jnp.inf)
        totals[g] = jnp.zeros(totals.shape[1:], jnp.float32)

        def score(t):
            tile = lax.dot_general(
                q_now[chosen(t)], kv[0, t], LAST, preferred_element_type=jnp.float32
            )
            tile = tile + bias[t]
            scores[t] = tile
            half = jnp.maximum(tile[:, :HD], tile[:, HD:])
            for i in range(2):
                penalty = jnp.where(chosen(t) == i, 0.0, -jnp.inf)
                maxima[i] = jnp.maximum(maxima[i], half + penalty)

        tiles(score)
        for i in range(2):
            top = jnp.max(maxima[i], axis=1, keepdims=True) * (SCALE * LOG2E)
            maxima[i] = jnp.broadcast_to(top, (BLOCK, HD))

        def weigh(t):
            tile = jnp.exp2(scores[t] * (SCALE * LOG2E) - twice(maxima[chosen(t)]))
            probs[g, :, tile_cols(t)] = tile.astype(jnp.bfloat16)
            half = tile[:, :HD] + tile[:, HD:]
            for i, flag in enumerate(flags(t)):
                totals[g, i] = totals[g, i] + half * flag

        tiles(weigh)
        for i in range(2):
            totals[g, i] = jnp.broadcast_to(
                1.0 / jnp.sum(totals[g, i], axis=1, keepdims=True), (BLOCK, HD)
            )

    def attend(g):
        both = jnp.dot(probs[g], wide_values[...], preferred_element_type=jnp.float32)
        for i in range(2):
            o_buf[g, i] = (
                both[:, i * HD : (i + 1) * HD] * totals[g, i]
            ).astype(jnp.bfloat16)
        send_out(o_buf, o_ref, g, 0)

    def prepare(g):
        drain(g_buf.at[g], wide_recv.at[1, g])
        for i in range(2):
            out_grad = g_buf[g, i].astype(jnp.float32) * totals[g, i]
            g_scaled[i] = out_grad.astype(jnp.bfloat16)
            row_sum = jnp.sum(o_buf[g, i].astype(jnp.float32) * out_grad, axis=1, keepdims=True)
            delta[i] = jnp.broadcast_to(row_sum, (BLOCK, HD))

    def value_grad(g, store):
        def step(t):
            store(
                t,
                lax.dot_general(
                    probs[g, :, tile_cols(t)],
                    g_scaled[chosen(t)],
                    FIRST,
                    preferred_element_type=jnp.float32,
                ),
            )

        tiles(step)

    def key_grad(g, store):
        def step(t):
            prob_grad = lax.dot_general(
                g_scaled[chosen(t)], kv[1, t], LAST, preferred_element_type=jnp.float32
            )
            score_grad = (
                probs[g, :, tile_cols(t)].astype(jnp.float32)
                * (prob_grad - twice(delta[chosen(t)]))
            ).astype(jnp.bfloat16)
            grads[g, :, tile_cols(t)] = score_grad
            store(
                t,
                lax.dot_general(
                    score_grad, q_buf[g, chosen(t)], FIRST, preferred_element_type=jnp.float32
                ),
            )

        tiles(step)

    def query_grad(g):
        both = jnp.dot(grads[g], wide_keys[...], preferred_element_type=jnp.float32)
        for i in range(2):
            dq_buf[g, i] = (
                both[:, i * HD : (i + 1) * HD] * SCALE
            ).astype(jnp.bfloat16)
        send_out(dq_buf, dq_ref, g, 1)

    sums[...] = jnp.zeros_like(sums)

    def keep(which):
        def store(t, value):
            sums[which, t] = sums[which, t] + value

        return store

    def finish(which, factor):
        def store(t, value):
            part[which, t] = ((sums[which, t] + value) * factor).astype(jnp.bfloat16)

        return store

    def send_parts(which):
        def send_part(peer_chip, core):
            peer = peer_chip * 2 + core
            remote(
                part.at[which, :, rows_of(peer)],
                arrived.at[pl.ds(me * slots, slots)],
                part_send,
                part_recv,
                peer,
                head,
            )

        loop(15, lambda r: send_part(lax.rem(chip + r + 1, 16), which))

        @pl.when(kind != which)
        def _():
            send_part(chip, which)

        @pl.when(kind == which)
        def _():
            pltpu.make_async_copy(
                part.at[which, :, rows_of(me)], arrived.at[pl.ds(me * slots, slots)], part_recv
            ).start()

    loop(slots, functools.partial(widen, wide_keys, 0))
    loop(GROUP, forward)
    drain(kv.at[1], list_recv.at[1])
    loop(slots, functools.partial(widen, wide_values, 1))
    loop(GROUP, attend)

    def one_head(g):
        prepare(g)
        value_grad(g, keep(1))
        key_grad(g, keep(0))

    loop(GROUP - 1, one_head)
    prepare(GROUP - 1)
    value_grad(GROUP - 1, finish(1, 1.0))
    send_parts(1)
    key_grad(GROUP - 1, finish(0, SCALE))
    send_parts(0)
    loop(GROUP, query_grad)

    nowhere = CTX * slots

    def make_table(place):
        block = order_ref[place]
        for step in range(SPAN):
            query = jnp.minimum(block + step, 2 * CTX - 1)
            spot = inverse_ref[query]
            device = lax.div(spot, 2)
            ahead = jnp.where(lax.rem(spot, 2) == 1, pair_of(device)[2], 0)
            listed = (block + step == query) & (first_ref[query] <= block)
            table[place * SPAN + step] = jnp.where(listed, device * slots + ahead + step, nowhere)

    loop(2 * CTX, make_table)
    arrived[nowhere] = jnp.zeros(arrived.shape[1:], arrived.dtype)
    drain(arrived.at[pl.ds(0, nowhere)], part_recv)

    def add_up(peer):
        for block in range(2):
            first = (peer * 2 + block) * SPAN
            total = arrived[table[first]].astype(jnp.float32)
            for step in range(1, SPAN):
                total = total + arrived[table[first + step]].astype(jnp.float32)
            summed[peer, block] = total.astype(summed.dtype)

    def send_sums(out_ref):
        def send_sum(r):
            peer = lax.rem(me + r + 1, CTX)
            add_up(peer)
            remote(
                summed.at[peer],
                out_ref.at[:, rows_of(me)],
                sum_send,
                sum_recv.at[kind],
                peer,
                head,
            )

        loop(CTX - 1, send_sum)
        add_up(me)
        pltpu.make_async_copy(
            summed.at[me], out_ref.at[:, rows_of(me)], sum_recv.at[kind]
        ).start()

    pl.when(kind == 0)(lambda: send_sums(dk_ref))
    pl.when(kind == 1)(lambda: send_sums(dv_ref))

    drain(pieces.at[pl.ds(0, ROWS - 1)], piece_send)

    @pl.when(lax.div(chip, 4) != lax.rem(head, 4))
    def _():
        drain(pieces.at[0], piece_send)

    for buf, which in ((q_buf, 0), (g_buf, 1)):
        for g in range(GROUP):
            drain(buf.at[g, 0], wide_send.at[which])
            drain(buf.at[g, 1, pl.ds(0, 3 * ROWS)], wide_send.at[which])
    drain(staged.at[pl.ds(0, CTX - 1)], list_send)
    drain(arrived.at[pl.ds(0, (CTX - 1) * slots)], part_send)
    drain(summed.at[pl.ds(0, CTX - 1)], sum_send)
    drain(o_buf, out_sem.at[0])
    drain(dq_buf, out_sem.at[1])
    drain(dk_ref, sum_recv.at[0])
    drain(dv_ref, sum_recv.at[1])


def fused(slots, identity, scalars, queries, keys, values, grads):
    docs = scalars[-1].shape[0]
    anywhere = pl.BlockSpec(memory_space=pl.ANY)
    small = pl.BlockSpec(memory_space=pltpu.SMEM)
    bf16, f32 = jnp.bfloat16, jnp.float32
    rows, wide = ROWS * HEADS, GROUP * HD
    dma = pltpu.SemaphoreType.DMA
    return pl.pallas_call(
        functools.partial(fused_kernel, slots, docs),
        out_shape=(
            jax.ShapeDtypeStruct((rows, wide), bf16),
            jax.ShapeDtypeStruct((rows, wide), bf16),
            jax.ShapeDtypeStruct((2, BLOCK, HD), bf16),
            jax.ShapeDtypeStruct((2, BLOCK, HD), bf16),
        ),
        in_specs=[small] * 4 + [anywhere] * 4,
        out_specs=[anywhere] * 4,
        scratch_shapes=[
            pltpu.SMEM((2 * CTX * SPAN,), jnp.int32),
            pltpu.VMEM((GROUP, 2, BLOCK, HD), bf16),
            pltpu.VMEM((GROUP, 2, BLOCK, HD), bf16),
            pltpu.VMEM((2, BLOCK, HD), bf16),
            pltpu.VMEM((2, BLOCK, HD), bf16),
            pltpu.VMEM((2, slots, BLOCK, HD), bf16),
            pltpu.VMEM((2 * CTX, PIECE, HD), bf16),
            pltpu.VMEM((CTX, slots, PIECE, HD), bf16),
            pltpu.VMEM((slots, BLOCK, BLOCK), f32),
            pltpu.VMEM((slots, BLOCK, BLOCK), f32),
            pltpu.VMEM((GROUP, BLOCK, slots * BLOCK), bf16),
            pltpu.VMEM((GROUP, BLOCK, slots * BLOCK), bf16),
            pltpu.VMEM((slots * BLOCK, 2 * HD), bf16),
            pltpu.VMEM((slots * BLOCK, 2 * HD), bf16),
            pltpu.VMEM((2, BLOCK, HD), f32),
            pltpu.VMEM((GROUP, 2, BLOCK, HD), f32),
            pltpu.VMEM((2, BLOCK, HD), f32),
            pltpu.VMEM((2, slots, BLOCK, HD), f32),
            pltpu.VMEM((2, slots, BLOCK, HD), bf16),
            pltpu.VMEM((GROUP, 2, BLOCK, HD), bf16),
            pltpu.VMEM((GROUP, 2, BLOCK, HD), bf16),
            pltpu.VMEM((CTX * slots + 1, PIECE, HD), bf16),
            pltpu.VMEM((CTX, 2, PIECE, HD), bf16),
            dma,
            dma,
            dma((2,)),
            dma((2, GROUP)),
            dma,
            dma((2,)),
            dma((2,)),
            dma,
            dma,
            dma,
            dma((2,)),
        ],
        compiler_params=pltpu.CompilerParams(
            collective_id=identity, has_side_effects=True, vmem_limit_bytes=52 << 20
        ),
        name="fused",
    )(*scalars, queries, keys, values, grads)


def on_device(queries, keys, values, grads, lengths, key_first, order):
    ids = jnp.arange(2 * CTX, dtype=jnp.int32)
    inverse = jnp.sum(jnp.where(order[None, :] == ids[:, None], ids[None, :], 0), axis=1)
    first = jnp.sum(jnp.where(order[:, None] == ids[None, :], key_first[None, :], 0), axis=1)
    counts = order - first + 1
    most = jnp.max(counts[0::2] + counts[1::2])

    def branch(slots, identity, queries, keys, values, grads):
        attended, query_grad, key_grad, value_grad = fused(
            slots, identity, (order, inverse, key_first, lengths), queries, keys, values, grads
        )
        rows = attended.shape[0]
        return attended, query_grad, key_grad.reshape(rows, HD), value_grad.reshape(rows, HD)

    return lax.cond(
        most <= 9,
        functools.partial(branch, 9, 0),
        functools.partial(branch, 2 * SPAN, 1),
        queries,
        keys,
        values,
        grads,
    )


def solution(mesh):
    return jax.shard_map(
        on_device,
        mesh=mesh,
        in_specs=(
            P(("ctx", "head"), None),
            P(("ctx", "head"), None),
            P(("ctx", "head"), None),
            P(("ctx", "head"), None),
            P(),
            P(),
            P(),
        ),
        out_specs=(P("ctx", "head"), P("ctx", "head"), P("ctx", "head"), P("ctx", "head")),
        check_vma=False,
    )
```

```python
import functools

import jax
import jax.numpy as jnp
from jax import lax
from jax.experimental import pallas as pl
from jax.experimental.pallas import tpu as pltpu
from jax.sharding import PartitionSpec as P

HD = 128
BLOCK = 256
SPAN = 7
CTX = 32
HEADS = 8
GROUP = 4
ROWS = 64
PIECE = 16
MESH = pl.DeviceIdType.MESH
LOG2E = 1.4426950408889634
SCALE = HD**-0.5
AHEAD = 4
EARLY = 2
LAST = (((1,), (1,)), ((), ()))
FIRST = (((0,), (0,)), ((), ()))


def drain(ref, sem):
    pltpu.make_async_copy(ref, ref, sem).wait()


def loop(count, body):
    def step(index, carry):
        body(index)
        return carry

    lax.fori_loop(0, count, step, 0)


def greet(me, head):
    barrier = pltpu.get_barrier_semaphore()
    chip = lax.div(me, 2)

    def signal(ctx, z):
        pl.semaphore_signal(barrier, inc=1, device_id=(ctx, z), device_id_type=MESH)

    loop(CTX - 1, lambda r: signal(lax.rem(me + r + 1, CTX), head))
    loop(HEADS - 1, lambda r: signal(me, lax.rem(head + r + 1, HEADS)))
    for half in range(2):
        source = half * 4 + lax.div(chip, 4)
        loop(CTX - 1, lambda r: signal(lax.rem(me + r + 1, CTX), source))

        @pl.when(source != head)
        def _():
            signal(me, source)

    apart = lax.rem(lax.div(chip, 4) + 4 - lax.rem(head, 4), 4)
    pl.semaphore_wait(barrier, CTX - 1 + HEADS - 1 + 2 * CTX - 1 + lax.div(apart + 3, 4))


def fused_kernel(
    slots,
    docs,
    order_ref,
    inverse_ref,
    first_ref,
    lengths_ref,
    q_ref,
    k_ref,
    v_ref,
    g_ref,
    o_ref,
    dq_ref,
    dk_ref,
    dv_ref,
    table,
    q_buf,
    g_buf,
    g_scaled,
    turned,
    o_turned,
    kv,
    pieces,
    staged,
    bias,
    scores,
    probs,
    grads,
    wide_keys,
    wide_values,
    maxima,
    totals,
    inverses,
    inverse_rows,
    delta,
    sums,
    part,
    o_buf,
    dq_buf,
    arrived,
    summed,
    landed,
    piece_send,
    piece_recv,
    wide_send,
    wide_recv,
    list_send,
    list_recv,
    out_sem,
    part_send,
    part_recv,
    sum_send,
    sum_recv,
):
    me = lax.axis_index("ctx")
    head = lax.axis_index("head")
    chip, kind = lax.div(me, 2), lax.rem(me, 2)
    greet(me, head)

    def remote(src, dst, send, recv, ctx, z):
        pltpu.make_async_remote_copy(
            src_ref=src,
            dst_ref=dst,
            send_sem=send,
            recv_sem=recv,
            device_id=(ctx, z),
            device_id_type=MESH,
        ).start()

    pair = lax.div(head, 4)

    def send_pieces(which):
        ref = (k_ref, v_ref)[which]
        slot = pieces.at[me * 2 + pair]

        def piece(p, z):
            rows = pl.ds(pl.multiple_of(p * PIECE, PIECE), PIECE)
            return ref.at[rows, pl.ds(pl.multiple_of(z * HD, HD), HD)]

        def target(p):
            return (lax.rem(head, 4) * 4 + p) * 2 + which

        def send_piece(r):
            p, z = lax.rem(r, 4), lax.rem(head + lax.div(r, 4) + 1, HEADS)
            remote(piece(p, z), slot, piece_send, piece_recv, target(p), z)

        loop(4 * (HEADS - 1), send_piece)
        for p in range(4):

            @pl.when(target(p) != me)
            def _(p=p):
                remote(piece(p, head), slot, piece_send, piece_recv, target(p), head)

            @pl.when(target(p) == me)
            def _(p=p):
                pltpu.make_async_copy(piece(p, head), slot, piece_recv).start()

    send_pieces(0)
    send_pieces(1)

    my_rows = pl.ds(pl.multiple_of(lax.rem(head, 4) * ROWS, ROWS), ROWS)

    def columns(z, g):
        return pl.ds(pl.multiple_of(z * GROUP * HD + g * HD, HD), HD)

    def send_chunk(chunk):
        which, g = divmod(chunk, GROUP)
        ref, buf = ((q_ref, q_buf), (g_ref, g_buf))[which]

        def send_wide(r):
            z = lax.rem(head + r + 1, HEADS)
            remote(
                ref.at[:, columns(z, g)],
                buf.at[g, pair, my_rows],
                wide_send.at[which],
                wide_recv.at[which, g],
                me,
                z,
            )

        loop(HEADS - 1, send_wide)
        pltpu.make_async_copy(
            ref.at[:, columns(head, g)], buf.at[g, pair, my_rows], wide_recv.at[which, g]
        ).start()

    def take_chunk(chunk):
        which, g = divmod(chunk, GROUP)
        drain((q_buf, g_buf)[which].at[g], wide_recv.at[which, g])
        if chunk + AHEAD < 2 * GROUP:
            send_chunk(chunk + AHEAD)

    for chunk in range(AHEAD):
        send_chunk(chunk)

    rows = lax.broadcasted_iota(jnp.int32, (BLOCK, BLOCK), 0)
    cols = lax.broadcasted_iota(jnp.int32, (BLOCK, BLOCK), 1)

    def pair_of(device):
        block_a, block_b = order_ref[2 * device], order_ref[2 * device + 1]
        return block_a, block_b, block_a - first_ref[block_a] + 1

    block_a, block_b, count_a = pair_of(me)
    count_b = block_b - first_ref[block_b] + 1

    def belongs(t):
        return (t == 1) | (t > count_a)

    def chosen(t):
        return belongs(t).astype(jnp.int32)

    def make_bias(t):
        late = belongs(t)
        block = jnp.where(late, block_b, block_a)
        back = jnp.where(t < 2, 0, jnp.where(late, t - count_a, t - 1))
        reach = jnp.where(t < count_a + count_b, back * BLOCK, -2 * BLOCK)
        low = jnp.zeros((BLOCK, BLOCK), jnp.int32)
        end = 0
        for doc in range(docs - 1):
            end = end + lengths_ref[doc]
            low = jnp.where(cols + block * BLOCK >= end, end, low)
        allowed = (rows + (block - back) * BLOCK >= low) & (rows - cols <= reach)
        bias[t] = jnp.where(allowed, 0.0, -jnp.inf)

    def rows_of(device):
        return pl.ds(pl.multiple_of(lax.div(device, 2) * PIECE, PIECE), PIECE)

    def send_lists():
        def stage(peer):
            first_block, second_block, first_count = pair_of(peer)
            for slot in range(slots):
                if slot < 2:
                    wanted = (first_block, second_block)[slot]
                else:
                    wanted = jnp.where(
                        slot <= first_count,
                        first_block - slot + 1,
                        second_block - slot + first_count,
                    )
                staged[peer, slot] = pieces[inverse_ref[jnp.maximum(wanted, 0)]]

        def send_list(r):
            peer = lax.rem(me + r + 1, CTX)
            stage(peer)
            remote(
                staged.at[peer],
                kv.at[kind, :, rows_of(me)],
                list_send,
                list_recv.at[kind],
                peer,
                head,
            )

        loop(CTX - 1, send_list)
        stage(me)
        pltpu.make_async_copy(
            staged.at[me], kv.at[kind, :, rows_of(me)], list_recv.at[kind]
        ).start()

    def first_round():
        drain(pieces, piece_recv)
        send_lists()

    pl.when(kind == 0)(first_round)
    take_chunk(0)
    loop(slots, make_bias)
    take_chunk(1)
    drain(kv.at[0], list_recv.at[0])

    def second_round():
        drain(pieces, piece_recv)
        send_lists()

    pl.when(kind == 1)(second_round)

    zeros = jnp.zeros((HD, BLOCK), jnp.bfloat16)

    def widen(wide, which, t):
        turned = kv[which, t].T
        for i, flag in enumerate((~belongs(t), belongs(t))):
            wide[i * HD : (i + 1) * HD, tile_cols(t)] = jnp.where(flag, turned, zeros)

    unroll = 3 if slots % 3 == 0 else 2

    def tiles(body):
        def several(index):
            for u in range(unroll):
                body(index * unroll + u)

        loop(slots // unroll, several)

    def tile_cols(t):
        return pl.ds(pl.multiple_of(t * BLOCK, BLOCK), BLOCK)

    def fold(tile, combine):
        height = tile.shape[0]
        while height > 8:
            height //= 2
            tile = combine(tile[:height], tile[height:])
        return tile

    def send_out(buf, ref, g, which):
        for i in range(2):
            pltpu.make_async_copy(
                buf.at[g, i],
                ref.at[pl.ds(i * BLOCK, BLOCK), pl.ds(pl.multiple_of(g * HD, HD), HD)],
                out_sem.at[which],
            ).start()

    def forward(g):
        for i in range(2):
            turned[i] = q_buf[g, i].T
        maxima[...] = jnp.full_like(maxima, -jnp.inf)
        totals[...] = jnp.zeros_like(totals)

        def score(t):
            tile = jnp.dot(kv[0, t], turned[chosen(t)], preferred_element_type=jnp.float32)
            tile = tile + bias[t]
            scores[t] = tile
            top = fold(tile, jnp.maximum)
            for i in range(2):
                penalty = jnp.where(chosen(t) == i, 0.0, -jnp.inf)
                maxima[i] = jnp.maximum(maxima[i], top + penalty)

        tiles(score)
        for i in range(2):
            top = jnp.max(maxima[i], axis=0, keepdims=True) * (SCALE * LOG2E)
            maxima[i] = jnp.broadcast_to(top, (8, BLOCK))

        def weigh(t):
            tile = jnp.exp2(scores[t] * (SCALE * LOG2E) - maxima[chosen(t), :1])
            probs[g, tile_cols(t)] = tile.astype(jnp.bfloat16)
            part_sum = fold(tile, jnp.add)
            late = belongs(t).astype(jnp.float32)
            for i, flag in enumerate((1.0 - late, late)):
                totals[i] = totals[i] + part_sum * flag

        tiles(weigh)
        for i in range(2):
            inverse = 1.0 / jnp.sum(totals[i], axis=0, keepdims=True)
            inverses[g, i] = jnp.broadcast_to(inverse, (8, BLOCK))
            inverse_rows[g, i] = jnp.broadcast_to(inverse, (HD, BLOCK)).T

    def attend(g):
        both = jnp.dot(wide_values[...], probs[g], preferred_element_type=jnp.float32)
        for i in range(2):
            result = both[i * HD : (i + 1) * HD] * inverses[g, i, :1]
            o_turned[g, i] = result.astype(jnp.bfloat16)
            o_buf[g, i] = result.T.astype(jnp.bfloat16)
        send_out(o_buf, o_ref, g, 0)

    def prepare(g):
        for i in range(2):
            scaled = (g_buf[g, i].astype(jnp.float32) * inverse_rows[g, i]).astype(jnp.bfloat16)
            g_scaled[g, i] = scaled

    def turn(g):
        for i in range(2):
            turned[i] = g_scaled[g, i].T
            product = o_turned[g, i].astype(jnp.float32) * turned[i].astype(jnp.float32)
            total = jnp.sum(fold(product, jnp.add), axis=0, keepdims=True)
            delta[i] = jnp.broadcast_to(total, (8, BLOCK))

    def value_grad(g, store):
        def step(t):
            store(
                t,
                jnp.dot(
                    probs[g, tile_cols(t)],
                    g_scaled[g, chosen(t)],
                    preferred_element_type=jnp.float32,
                ),
            )

        tiles(step)

    def key_grad(g, store):
        def step(t):
            prob_grad = jnp.dot(kv[1, t], turned[chosen(t)], preferred_element_type=jnp.float32)
            score_grad = (
                probs[g, tile_cols(t)].astype(jnp.float32)
                * (prob_grad - delta[chosen(t), :1])
            ).astype(jnp.bfloat16)
            grads[g, tile_cols(t)] = score_grad
            store(
                t, jnp.dot(score_grad, q_buf[g, chosen(t)], preferred_element_type=jnp.float32)
            )

        tiles(step)

    def query_grad(g):
        both = jnp.dot(wide_keys[...], grads[g], preferred_element_type=jnp.float32)
        for i in range(2):
            dq_buf[g, i] = (both[i * HD : (i + 1) * HD] * SCALE).T.astype(jnp.bfloat16)
        send_out(dq_buf, dq_ref, g, 1)

    sums[...] = jnp.zeros_like(sums)
    others = slots - 2

    def keep(which):
        def store(t, value):
            sums[which, t] = sums[which, t] + value

        return store

    def finish(which, factor):
        def store(t, value):
            part[which, t] = ((sums[which, t] + value) * factor).astype(jnp.bfloat16)

        return store

    def send_parts(which):
        def send_part(peer_chip, core):
            peer = peer_chip * 2 + core
            remote(
                part.at[which, pl.ds(2, others), rows_of(peer)],
                arrived.at[pl.ds(me * others, others)],
                part_send,
                part_recv,
                peer,
                head,
            )

        loop(15, lambda r: send_part(lax.rem(chip + r + 1, 16), which))

        @pl.when(kind != which)
        def _():
            send_part(chip, which)

        @pl.when(kind == which)
        def _():
            pltpu.make_async_copy(
                part.at[which, pl.ds(2, others), rows_of(me)],
                arrived.at[pl.ds(me * others, others)],
                part_recv,
            ).start()

    loop(slots, functools.partial(widen, wide_keys, 0))
    for g in range(GROUP):
        if g >= 2:
            take_chunk(g)
        forward(g)
    for g in range(GROUP - 1):
        take_chunk(GROUP + g)
        prepare(g)
        value_grad(g, keep(1))
    drain(kv.at[1], list_recv.at[1])
    loop(slots, functools.partial(widen, wide_values, 1))
    loop(GROUP, attend)

    def early(g):
        turn(g)
        key_grad(g, keep(0))

    loop(EARLY, early)
    take_chunk(2 * GROUP - 1)
    prepare(GROUP - 1)
    value_grad(GROUP - 1, finish(1, 1.0))
    send_parts(1)
    loop(GROUP - 1 - EARLY, lambda g: early(g + EARLY))
    turn(GROUP - 1)
    key_grad(GROUP - 1, finish(0, SCALE))
    send_parts(0)
    loop(GROUP, query_grad)

    nowhere = CTX * others

    def make_table(place):
        block = order_ref[place]
        for step in range(SPAN - 1):
            query = jnp.minimum(block + step + 1, 2 * CTX - 1)
            spot = inverse_ref[query]
            device = lax.div(spot, 2)
            ahead = jnp.where(lax.rem(spot, 2) == 1, pair_of(device)[2] - 1, 0)
            listed = (block + step + 1 == query) & (first_ref[query] <= block)
            table[place * SPAN + step] = jnp.where(listed, device * others + ahead + step, nowhere)

    loop(2 * CTX, make_table)
    arrived[nowhere] = jnp.zeros(arrived.shape[1:], arrived.dtype)
    drain(arrived.at[pl.ds(0, nowhere)], part_recv)

    def add_up(peer):
        for block in range(2):
            first = (peer * 2 + block) * SPAN
            total = arrived[table[first]].astype(jnp.float32)
            for step in range(1, SPAN - 1):
                total = total + arrived[table[first + step]].astype(jnp.float32)
            summed[peer, block] = total.astype(summed.dtype)

    def send_sum(r):
        peer = lax.rem(me + r + 1, CTX)
        add_up(peer)
        remote(
            summed.at[peer],
            landed.at[kind, :, rows_of(me)],
            sum_send,
            sum_recv.at[kind],
            peer,
            head,
        )

    loop(CTX - 1, send_sum)
    add_up(me)
    pltpu.make_async_copy(
        summed.at[me], landed.at[kind, :, rows_of(me)], sum_recv.at[kind]
    ).start()

    drain(pieces.at[pl.ds(0, ROWS - 1)], piece_send)

    @pl.when(lax.div(chip, 4) != lax.rem(head, 4))
    def _():
        drain(pieces.at[0], piece_send)

    for buf, which in ((q_buf, 0), (g_buf, 1)):
        for g in range(GROUP):
            drain(buf.at[g, 0], wide_send.at[which])
            drain(buf.at[g, 1, pl.ds(0, 3 * ROWS)], wide_send.at[which])
    drain(staged.at[pl.ds(0, CTX - 1)], list_send)
    drain(arrived.at[pl.ds(0, (CTX - 1) * others)], part_send)
    drain(summed.at[pl.ds(0, CTX - 1)], sum_send)
    drain(o_buf, out_sem.at[0])
    drain(dq_buf, out_sem.at[1])
    for which, out_ref in ((1, dv_ref), (0, dk_ref)):
        drain(landed.at[which], sum_recv.at[which])
        for i in range(2):
            total = landed[which, i].astype(jnp.float32) + part[which, i].astype(jnp.float32)
            out_ref[i] = total.astype(jnp.bfloat16)


def fused(slots, identity, scalars, queries, keys, values, grads):
    docs = scalars[-1].shape[0]
    anywhere = pl.BlockSpec(memory_space=pl.ANY)
    small = pl.BlockSpec(memory_space=pltpu.SMEM)
    bf16, f32 = jnp.bfloat16, jnp.float32
    rows, wide = ROWS * HEADS, GROUP * HD
    dma = pltpu.SemaphoreType.DMA
    return pl.pallas_call(
        functools.partial(fused_kernel, slots, docs),
        out_shape=(
            jax.ShapeDtypeStruct((rows, wide), bf16),
            jax.ShapeDtypeStruct((rows, wide), bf16),
            jax.ShapeDtypeStruct((2, BLOCK, HD), bf16),
            jax.ShapeDtypeStruct((2, BLOCK, HD), bf16),
        ),
        in_specs=[small] * 4 + [anywhere] * 4,
        out_specs=[anywhere] * 2 + [pl.BlockSpec(memory_space=pltpu.VMEM)] * 2,
        scratch_shapes=[
            pltpu.SMEM((2 * CTX * SPAN,), jnp.int32),
            pltpu.VMEM((GROUP, 2, BLOCK, HD), bf16),
            pltpu.VMEM((GROUP, 2, BLOCK, HD), bf16),
            pltpu.VMEM((GROUP, 2, BLOCK, HD), bf16),
            pltpu.VMEM((2, HD, BLOCK), bf16),
            pltpu.VMEM((GROUP, 2, HD, BLOCK), bf16),
            pltpu.VMEM((2, slots, BLOCK, HD), bf16),
            pltpu.VMEM((2 * CTX, PIECE, HD), bf16),
            pltpu.VMEM((CTX, slots, PIECE, HD), bf16),
            pltpu.VMEM((slots, BLOCK, BLOCK), f32),
            pltpu.VMEM((slots, BLOCK, BLOCK), f32),
            pltpu.VMEM((GROUP, slots * BLOCK, BLOCK), bf16),
            pltpu.VMEM((GROUP, slots * BLOCK, BLOCK), bf16),
            pltpu.VMEM((2 * HD, slots * BLOCK), bf16),
            pltpu.VMEM((2 * HD, slots * BLOCK), bf16),
            pltpu.VMEM((2, 8, BLOCK), f32),
            pltpu.VMEM((2, 8, BLOCK), f32),
            pltpu.VMEM((GROUP, 2, 8, BLOCK), f32),
            pltpu.VMEM((GROUP, 2, BLOCK, HD), f32),
            pltpu.VMEM((2, 8, BLOCK), f32),
            pltpu.VMEM((2, slots, BLOCK, HD), f32),
            pltpu.VMEM((2, slots, BLOCK, HD), bf16),
            pltpu.VMEM((GROUP, 2, BLOCK, HD), bf16),
            pltpu.VMEM((GROUP, 2, BLOCK, HD), bf16),
            pltpu.VMEM((CTX * (slots - 2) + 1, PIECE, HD), bf16),
            pltpu.VMEM((CTX, 2, PIECE, HD), bf16),
            pltpu.VMEM((2, 2, BLOCK, HD), bf16),
            dma,
            dma,
            dma((2,)),
            dma((2, GROUP)),
            dma,
            dma((2,)),
            dma((2,)),
            dma,
            dma,
            dma,
            dma((2,)),
        ],
        compiler_params=pltpu.CompilerParams(
            collective_id=identity, has_side_effects=True, vmem_limit_bytes=52 << 20
        ),
        name="fused",
    )(*scalars, queries, keys, values, grads)


def deliver_kernel(*refs):
    half = len(refs) // 2
    copies = [
        pltpu.make_async_copy(refs[i], refs[half + i], refs[2 * half].at[i]) for i in range(half)
    ]
    for copy in copies:
        copy.start()
    for copy in copies:
        copy.wait()


def deliver(*results):
    anywhere = pl.BlockSpec(memory_space=pl.ANY)
    return pl.pallas_call(
        deliver_kernel,
        out_shape=tuple(jax.ShapeDtypeStruct(r.shape, r.dtype) for r in results),
        in_specs=[anywhere] * len(results),
        out_specs=[anywhere] * len(results),
        scratch_shapes=[pltpu.SemaphoreType.DMA((len(results),))],
        name="deliver",
    )(*results)


def on_device(queries, keys, values, grads, lengths, key_first, order):
    ids = jnp.arange(2 * CTX, dtype=jnp.int32)
    inverse = jnp.sum(jnp.where(order[None, :] == ids[:, None], ids[None, :], 0), axis=1)
    first = jnp.sum(jnp.where(order[:, None] == ids[None, :], key_first[None, :], 0), axis=1)
    counts = order - first + 1
    most = jnp.max(counts[0::2] + counts[1::2])

    def branch(slots, identity, queries, keys, values, grads):
        attended, query_grad, key_grad, value_grad = fused(
            slots, identity, (order, inverse, key_first, lengths), queries, keys, values, grads
        )
        rows = attended.shape[0]
        return attended, query_grad, key_grad.reshape(rows, HD), value_grad.reshape(rows, HD)

    results = lax.cond(
        most <= 9,
        functools.partial(branch, 9, 0),
        functools.partial(branch, 2 * SPAN, 1),
        queries,
        keys,
        values,
        grads,
    )
    return deliver(*results)


def solution(mesh):
    return jax.shard_map(
        on_device,
        mesh=mesh,
        in_specs=(
            P(("ctx", "head"), None),
            P(("ctx", "head"), None),
            P(("ctx", "head"), None),
            P(("ctx", "head"), None),
            P(),
            P(),
            P(),
        ),
        out_specs=(P("ctx", "head"), P("ctx", "head"), P("ctx", "head"), P("ctx", "head")),
        check_vma=False,
    )
```

```python
import functools

import jax
import jax.numpy as jnp
from jax import lax
from jax.experimental import pallas as pl
from jax.experimental.pallas import tpu as pltpu
from jax.sharding import PartitionSpec as P

HD = 128
BLOCK = 256
SPAN = 7
SHORT = 9
CTX = 32
HEADS = 8
GROUP = 4
ROWS = 64
PIECE = 16
MESH = pl.DeviceIdType.MESH
LOG2E = 1.4426950408889634
SCALE = HD**-0.5
AHEAD = 6
EARLY = 2
LAST = (((1,), (1,)), ((), ()))
FIRST = (((0,), (0,)), ((), ()))


def drain(ref, sem):
    pltpu.make_async_copy(ref, ref, sem).wait()


def loop(count, body):
    def step(index, carry):
        body(index)
        return carry

    lax.fori_loop(0, count, step, 0)


def grouped(count, ready, send):
    def several(first, size):
        for u in range(size):
            ready(first + u)
        for u in range(size):
            send(first + u)

    loop(count // 4, lambda index: several(index * 4, 4))
    several(count // 4 * 4, count % 4)


def greet(me, head):
    barrier = pltpu.get_barrier_semaphore()
    chip = lax.div(me, 2)

    def signal(ctx, z):
        pl.semaphore_signal(barrier, inc=1, device_id=(ctx, z), device_id_type=MESH)

    loop(CTX - 1, lambda r: signal(lax.rem(me + r + 1, CTX), head))
    loop(HEADS - 1, lambda r: signal(me, lax.rem(head + r + 1, HEADS)))
    for half in range(2):
        source = half * 4 + lax.div(chip, 4)
        loop(CTX - 1, lambda r: signal(lax.rem(me + r + 1, CTX), source))

        @pl.when(source != head)
        def _():
            signal(me, source)

    apart = lax.rem(lax.div(chip, 4) + 4 - lax.rem(head, 4), 4)
    pl.semaphore_wait(barrier, CTX - 1 + HEADS - 1 + 2 * CTX - 1 + lax.div(apart + 3, 4))


def fused_kernel(
    slots,
    docs,
    order_ref,
    inverse_ref,
    first_ref,
    lengths_ref,
    q_ref,
    k_ref,
    v_ref,
    g_ref,
    o_ref,
    dq_ref,
    dk_ref,
    dv_ref,
    most_ref,
    table,
    q_buf,
    g_buf,
    g_scaled,
    turned,
    o_turned,
    kv,
    pieces,
    staged,
    bias,
    scores,
    probs,
    grads,
    wide_keys,
    wide_values,
    maxima,
    totals,
    inverses,
    inverse_rows,
    delta,
    sums,
    part,
    o_buf,
    dq_buf,
    arrived,
    summed,
    landed,
    piece_send,
    piece_recv,
    wide_send,
    wide_recv,
    list_send,
    list_recv,
    out_sem,
    part_send,
    part_recv,
    sum_send,
    sum_recv,
):
    me = lax.axis_index("ctx")
    head = lax.axis_index("head")
    chip, kind = lax.div(me, 2), lax.rem(me, 2)
    greet(me, head)

    def remote(src, dst, send, recv, ctx, z):
        pltpu.make_async_remote_copy(
            src_ref=src,
            dst_ref=dst,
            send_sem=send,
            recv_sem=recv,
            device_id=(ctx, z),
            device_id_type=MESH,
        ).start()

    pair = lax.div(head, 4)

    def send_pieces(which):
        ref = (k_ref, v_ref)[which]
        slot = pieces.at[me * 2 + pair]

        def piece(p, z):
            rows = pl.ds(pl.multiple_of(p * PIECE, PIECE), PIECE)
            return ref.at[rows, pl.ds(pl.multiple_of(z * HD, HD), HD)]

        def target(p):
            return (lax.rem(head, 4) * 4 + p) * 2 + which

        def send_piece(r):
            p, z = lax.rem(r, 4), lax.rem(head + lax.div(r, 4) + 1, HEADS)
            remote(piece(p, z), slot, piece_send, piece_recv, target(p), z)

        loop(4 * (HEADS - 1), send_piece)
        for p in range(4):

            @pl.when(target(p) != me)
            def _(p=p):
                remote(piece(p, head), slot, piece_send, piece_recv, target(p), head)

            @pl.when(target(p) == me)
            def _(p=p):
                pltpu.make_async_copy(piece(p, head), slot, piece_recv).start()

    send_pieces(0)
    send_pieces(1)

    my_rows = pl.ds(pl.multiple_of(lax.rem(head, 4) * ROWS, ROWS), ROWS)

    def columns(z, g):
        return pl.ds(pl.multiple_of(z * GROUP * HD + g * HD, HD), HD)

    def send_chunk(chunk):
        which, g = divmod(chunk, GROUP)
        ref, buf = ((q_ref, q_buf), (g_ref, g_buf))[which]

        def send_wide(r):
            z = lax.rem(head + r + 1, HEADS)
            remote(
                ref.at[:, columns(z, g)],
                buf.at[g, pair, my_rows],
                wide_send.at[which],
                wide_recv.at[which, g],
                me,
                z,
            )

        loop(HEADS - 1, send_wide)
        pltpu.make_async_copy(
            ref.at[:, columns(head, g)], buf.at[g, pair, my_rows], wide_recv.at[which, g]
        ).start()

    def take_chunk(chunk):
        which, g = divmod(chunk, GROUP)
        drain((q_buf, g_buf)[which].at[g], wide_recv.at[which, g])
        if chunk + AHEAD < 2 * GROUP:
            send_chunk(chunk + AHEAD)

    for chunk in range(AHEAD):
        send_chunk(chunk)

    rows = lax.broadcasted_iota(jnp.int32, (BLOCK, BLOCK), 0)
    cols = lax.broadcasted_iota(jnp.int32, (BLOCK, BLOCK), 1)

    def pair_of(device):
        block_a, block_b = order_ref[2 * device], order_ref[2 * device + 1]
        return block_a, block_b, block_a - first_ref[block_a] + 1

    block_a, block_b, count_a = pair_of(me)
    count_b = block_b - first_ref[block_b] + 1

    def belongs(t):
        return (t == 1) | (t > count_a)

    def chosen(t):
        return belongs(t).astype(jnp.int32)

    def make_bias(t):
        late = belongs(t)
        block = jnp.where(late, block_b, block_a)
        back = jnp.where(t < 2, 0, jnp.where(late, t - count_a, t - 1))
        reach = jnp.where(t < count_a + count_b, back * BLOCK, -2 * BLOCK)
        low = jnp.zeros((BLOCK, BLOCK), jnp.int32)
        end = 0
        for doc in range(docs - 1):
            end = end + lengths_ref[doc]
            low = jnp.where(cols + block * BLOCK >= end, end, low)
        allowed = (rows + (block - back) * BLOCK >= low) & (rows - cols <= reach)
        bias[t] = jnp.where(allowed, 0.0, -jnp.inf)

    def rows_of(device):
        return pl.ds(pl.multiple_of(lax.div(device, 2) * PIECE, PIECE), PIECE)

    def send_lists():
        def stage(peer):
            first_block, second_block, first_count = pair_of(peer)
            for slot in range(slots):
                if slot < 2:
                    wanted = (first_block, second_block)[slot]
                else:
                    wanted = jnp.where(
                        slot <= first_count,
                        first_block - slot + 1,
                        second_block - slot + first_count,
                    )
                staged[peer, slot] = pieces[inverse_ref[jnp.maximum(wanted, 0)]]

        def send_list(r):
            peer = lax.rem(me + r + 1, CTX)
            remote(
                staged.at[peer],
                kv.at[kind, :, rows_of(me)],
                list_send,
                list_recv.at[kind],
                peer,
                head,
            )

        grouped(CTX - 1, lambda r: stage(lax.rem(me + r + 1, CTX)), send_list)
        stage(me)
        pltpu.make_async_copy(
            staged.at[me], kv.at[kind, :, rows_of(me)], list_recv.at[kind]
        ).start()

    def first_round():
        drain(pieces, piece_recv)
        send_lists()

    pl.when(kind == 0)(first_round)
    take_chunk(0)
    loop(slots, make_bias)
    take_chunk(1)

    def tile_count(device, most):
        first_block, second_block, first_count = pair_of(device)
        return jnp.maximum(most, first_count + second_block - first_ref[second_block] + 1)

    most_ref[0] = lax.fori_loop(0, CTX, tile_count, 0)
    drain(kv.at[0], list_recv.at[0])

    def second_round():
        drain(pieces, piece_recv)
        send_lists()

    pl.when(kind == 1)(second_round)

    zeros = jnp.zeros((HD, BLOCK), jnp.bfloat16)

    def widen(wide, which, t):
        turned = kv[which, t].T
        for i, flag in enumerate((~belongs(t), belongs(t))):
            wide[i * HD : (i + 1) * HD, tile_cols(t)] = jnp.where(flag, turned, zeros)

    unroll = 3 if slots % 3 == 0 else 2

    def tiles(body):
        def several(index):
            for u in range(unroll):
                body(index * unroll + u)

        loop(slots // unroll, several)

    def tile_cols(t):
        return pl.ds(pl.multiple_of(t * BLOCK, BLOCK), BLOCK)

    def fold(tile, combine):
        height = tile.shape[0]
        while height > 8:
            height //= 2
            tile = combine(tile[:height], tile[height:])
        return tile

    def send_out(buf, ref, g, which):
        for i in range(2):
            pltpu.make_async_copy(
                buf.at[g, i],
                ref.at[pl.ds(i * BLOCK, BLOCK), pl.ds(pl.multiple_of(g * HD, HD), HD)],
                out_sem.at[which],
            ).start()

    def forward(g):
        for i in range(2):
            turned[i] = q_buf[g, i].T
        maxima[...] = jnp.full_like(maxima, -jnp.inf)
        totals[...] = jnp.zeros_like(totals)

        def score(t):
            tile = jnp.dot(kv[0, t], turned[chosen(t)], preferred_element_type=jnp.float32)
            tile = tile + bias[t]
            scores[t] = tile
            top = fold(tile, jnp.maximum)
            for i in range(2):
                penalty = jnp.where(chosen(t) == i, 0.0, -jnp.inf)
                maxima[i] = jnp.maximum(maxima[i], top + penalty)

        tiles(score)
        for i in range(2):
            top = jnp.max(maxima[i], axis=0, keepdims=True) * (SCALE * LOG2E)
            maxima[i] = jnp.broadcast_to(top, (8, BLOCK))

        def weigh(t):
            tile = jnp.exp2(scores[t] * (SCALE * LOG2E) - maxima[chosen(t), :1])
            probs[g, tile_cols(t)] = tile.astype(jnp.bfloat16)
            part_sum = fold(tile, jnp.add)
            late = belongs(t).astype(jnp.float32)
            for i, flag in enumerate((1.0 - late, late)):
                totals[i] = totals[i] + part_sum * flag

        tiles(weigh)
        for i in range(2):
            inverse = 1.0 / jnp.sum(totals[i], axis=0, keepdims=True)
            inverses[g, i] = jnp.broadcast_to(inverse, (8, BLOCK))
            inverse_rows[g, i] = jnp.broadcast_to(inverse, (HD, BLOCK)).T

    def attend(g):
        both = jnp.dot(wide_values[...], probs[g], preferred_element_type=jnp.float32)
        for i in range(2):
            result = both[i * HD : (i + 1) * HD] * inverses[g, i, :1]
            o_turned[g, i] = result.astype(jnp.bfloat16)
            o_buf[g, i] = result.T.astype(jnp.bfloat16)
        send_out(o_buf, o_ref, g, 0)

    def prepare(g):
        for i in range(2):
            scaled = (g_buf[g, i].astype(jnp.float32) * inverse_rows[g, i]).astype(jnp.bfloat16)
            g_scaled[g, i] = scaled

    def turn(g):
        for i in range(2):
            turned[i] = g_scaled[g, i].T
            product = o_turned[g, i].astype(jnp.float32) * turned[i].astype(jnp.float32)
            total = jnp.sum(fold(product, jnp.add), axis=0, keepdims=True)
            delta[i] = jnp.broadcast_to(total, (8, BLOCK))

    def value_grad(g, store):
        def step(t):
            store(
                t,
                jnp.dot(
                    probs[g, tile_cols(t)],
                    g_scaled[g, chosen(t)],
                    preferred_element_type=jnp.float32,
                ),
            )

        tiles(step)

    def key_grad(g, store):
        def step(t):
            prob_grad = jnp.dot(kv[1, t], turned[chosen(t)], preferred_element_type=jnp.float32)
            score_grad = (
                probs[g, tile_cols(t)].astype(jnp.float32)
                * (prob_grad - delta[chosen(t), :1])
            ).astype(jnp.bfloat16)
            grads[g, tile_cols(t)] = score_grad
            store(
                t, jnp.dot(score_grad, q_buf[g, chosen(t)], preferred_element_type=jnp.float32)
            )

        tiles(step)

    def query_grad(g):
        both = jnp.dot(wide_keys[...], grads[g], preferred_element_type=jnp.float32)
        for i in range(2):
            dq_buf[g, i] = (both[i * HD : (i + 1) * HD] * SCALE).T.astype(jnp.bfloat16)
        send_out(dq_buf, dq_ref, g, 1)

    sums[...] = jnp.zeros_like(sums)
    others = slots - 2

    def keep(which):
        def store(t, value):
            sums[which, t] = sums[which, t] + value

        return store

    def finish(which, factor):
        def store(t, value):
            part[which, t] = ((sums[which, t] + value) * factor).astype(jnp.bfloat16)

        return store

    def send_parts(which):
        def send_part(peer_chip, core):
            peer = peer_chip * 2 + core
            remote(
                part.at[which, pl.ds(2, others), rows_of(peer)],
                arrived.at[pl.ds(me * others, others)],
                part_send,
                part_recv,
                peer,
                head,
            )

        loop(15, lambda r: send_part(lax.rem(chip + r + 1, 16), which))

        @pl.when(kind != which)
        def _():
            send_part(chip, which)

        @pl.when(kind == which)
        def _():
            pltpu.make_async_copy(
                part.at[which, pl.ds(2, others), rows_of(me)],
                arrived.at[pl.ds(me * others, others)],
                part_recv,
            ).start()

    loop(slots, functools.partial(widen, wide_keys, 0))
    for g in range(GROUP):
        if g >= 2:
            take_chunk(g)
        forward(g)
    for g in range(GROUP - 1):
        take_chunk(GROUP + g)
        prepare(g)
        value_grad(g, keep(1))
    drain(kv.at[1], list_recv.at[1])
    loop(slots, functools.partial(widen, wide_values, 1))
    loop(GROUP, attend)

    def early(g):
        turn(g)
        key_grad(g, keep(0))

    loop(EARLY, early)
    take_chunk(2 * GROUP - 1)
    prepare(GROUP - 1)
    value_grad(GROUP - 1, finish(1, 1.0))
    send_parts(1)
    loop(GROUP - 1 - EARLY, lambda g: early(g + EARLY))
    turn(GROUP - 1)
    key_grad(GROUP - 1, finish(0, SCALE))
    send_parts(0)
    loop(GROUP, query_grad)

    nowhere = CTX * others

    def make_table(place):
        block = order_ref[place]
        for step in range(SPAN - 1):
            query = jnp.minimum(block + step + 1, 2 * CTX - 1)
            spot = inverse_ref[query]
            device = lax.div(spot, 2)
            ahead = jnp.where(lax.rem(spot, 2) == 1, pair_of(device)[2] - 1, 0)
            listed = (block + step + 1 == query) & (first_ref[query] <= block)
            spot = jnp.minimum(device * others + ahead + step, nowhere)
            table[place * SPAN + step] = jnp.where(listed, spot, nowhere)

    loop(2 * CTX, make_table)
    arrived[nowhere] = jnp.zeros(arrived.shape[1:], arrived.dtype)
    drain(arrived.at[pl.ds(0, nowhere)], part_recv)

    def add_up(peer):
        for block in range(2):
            first = (peer * 2 + block) * SPAN
            total = arrived[table[first]].astype(jnp.float32)
            for step in range(1, SPAN - 1):
                total = total + arrived[table[first + step]].astype(jnp.float32)
            summed[peer, block] = total.astype(summed.dtype)

    def send_sum(r):
        peer = lax.rem(me + r + 1, CTX)
        remote(
            summed.at[peer],
            landed.at[kind, :, rows_of(me)],
            sum_send,
            sum_recv.at[kind],
            peer,
            head,
        )

    grouped(CTX - 1, lambda r: add_up(lax.rem(me + r + 1, CTX)), send_sum)
    add_up(me)
    pltpu.make_async_copy(
        summed.at[me], landed.at[kind, :, rows_of(me)], sum_recv.at[kind]
    ).start()

    drain(pieces.at[pl.ds(0, ROWS - 1)], piece_send)

    @pl.when(lax.div(chip, 4) != lax.rem(head, 4))
    def _():
        drain(pieces.at[0], piece_send)

    for buf, which in ((q_buf, 0), (g_buf, 1)):
        for g in range(GROUP):
            drain(buf.at[g, 0], wide_send.at[which])
            drain(buf.at[g, 1, pl.ds(0, 3 * ROWS)], wide_send.at[which])
    drain(staged.at[pl.ds(0, CTX - 1)], list_send)
    drain(arrived.at[pl.ds(0, (CTX - 1) * others)], part_send)
    drain(summed.at[pl.ds(0, CTX - 1)], sum_send)
    drain(o_buf, out_sem.at[0])
    drain(dq_buf, out_sem.at[1])
    for which, out_ref in ((1, dv_ref), (0, dk_ref)):
        drain(landed.at[which], sum_recv.at[which])
        for i in range(2):
            total = landed[which, i].astype(jnp.float32) + part[which, i].astype(jnp.float32)
            out_ref[i] = total.astype(jnp.bfloat16)


def fused(slots, identity, scalars, queries, keys, values, grads):
    docs = scalars[-1].shape[0]
    anywhere = pl.BlockSpec(memory_space=pl.ANY)
    small = pl.BlockSpec(memory_space=pltpu.SMEM)
    bf16, f32 = jnp.bfloat16, jnp.float32
    rows, wide = ROWS * HEADS, GROUP * HD
    dma = pltpu.SemaphoreType.DMA
    return pl.pallas_call(
        functools.partial(fused_kernel, slots, docs),
        out_shape=(
            jax.ShapeDtypeStruct((rows, wide), bf16),
            jax.ShapeDtypeStruct((rows, wide), bf16),
            jax.ShapeDtypeStruct((2, BLOCK, HD), bf16),
            jax.ShapeDtypeStruct((2, BLOCK, HD), bf16),
            jax.ShapeDtypeStruct((1,), jnp.int32),
        ),
        in_specs=[small] * 4 + [anywhere] * 4,
        out_specs=[anywhere] * 2 + [pl.BlockSpec(memory_space=pltpu.VMEM)] * 2 + [small],
        scratch_shapes=[
            pltpu.SMEM((2 * CTX * SPAN,), jnp.int32),
            pltpu.VMEM((GROUP, 2, BLOCK, HD), bf16),
            pltpu.VMEM((GROUP, 2, BLOCK, HD), bf16),
            pltpu.VMEM((GROUP, 2, BLOCK, HD), bf16),
            pltpu.VMEM((2, HD, BLOCK), bf16),
            pltpu.VMEM((GROUP, 2, HD, BLOCK), bf16),
            pltpu.VMEM((2, slots, BLOCK, HD), bf16),
            pltpu.VMEM((2 * CTX, PIECE, HD), bf16),
            pltpu.VMEM((CTX, slots, PIECE, HD), bf16),
            pltpu.VMEM((slots, BLOCK, BLOCK), f32),
            pltpu.VMEM((slots, BLOCK, BLOCK), f32),
            pltpu.VMEM((GROUP, slots * BLOCK, BLOCK), bf16),
            pltpu.VMEM((GROUP, slots * BLOCK, BLOCK), bf16),
            pltpu.VMEM((2 * HD, slots * BLOCK), bf16),
            pltpu.VMEM((2 * HD, slots * BLOCK), bf16),
            pltpu.VMEM((2, 8, BLOCK), f32),
            pltpu.VMEM((2, 8, BLOCK), f32),
            pltpu.VMEM((GROUP, 2, 8, BLOCK), f32),
            pltpu.VMEM((GROUP, 2, BLOCK, HD), f32),
            pltpu.VMEM((2, 8, BLOCK), f32),
            pltpu.VMEM((2, slots, BLOCK, HD), f32),
            pltpu.VMEM((2, slots, BLOCK, HD), bf16),
            pltpu.VMEM((GROUP, 2, BLOCK, HD), bf16),
            pltpu.VMEM((GROUP, 2, BLOCK, HD), bf16),
            pltpu.VMEM((CTX * (slots - 2) + 1, PIECE, HD), bf16),
            pltpu.VMEM((CTX, 2, PIECE, HD), bf16),
            pltpu.VMEM((2, 2, BLOCK, HD), bf16),
            dma,
            dma,
            dma((2,)),
            dma((2, GROUP)),
            dma,
            dma((2,)),
            dma((2,)),
            dma,
            dma,
            dma,
            dma((2,)),
        ],
        compiler_params=pltpu.CompilerParams(
            collective_id=identity, has_side_effects=True, vmem_limit_bytes=52 << 20
        ),
        name="fused",
    )(*scalars, queries, keys, values, grads)


def deliver_kernel(*refs):
    half = len(refs) // 2
    copies = [
        pltpu.make_async_copy(refs[i], refs[half + i], refs[2 * half].at[i]) for i in range(half)
    ]
    for copy in copies:
        copy.start()
    for copy in copies:
        copy.wait()


def deliver(*results):
    anywhere = pl.BlockSpec(memory_space=pl.ANY)
    return pl.pallas_call(
        deliver_kernel,
        out_shape=tuple(jax.ShapeDtypeStruct(r.shape, r.dtype) for r in results),
        in_specs=[anywhere] * len(results),
        out_specs=[anywhere] * len(results),
        scratch_shapes=[pltpu.SemaphoreType.DMA((len(results),))],
        name="deliver",
    )(*results)


def on_device(queries, keys, values, grads, lengths, key_first, order):
    ids = jnp.arange(2 * CTX, dtype=jnp.int32)
    inverse = jnp.sum(jnp.where(order[None, :] == ids[:, None], ids[None, :], 0), axis=1)
    scalars = (order, inverse, key_first, lengths)
    *results, most = fused(SHORT, 0, scalars, queries, keys, values, grads)

    def deliver_results(*results):
        rows = results[0].shape[0]
        return deliver(*(r.reshape(rows, r.shape[-1]) for r in results))

    def enough(results, arrays):
        return deliver_results(*results)

    def general(results, arrays):
        return deliver_results(*fused(2 * SPAN, 1, scalars, *arrays)[:4])

    return lax.cond(
        most[0] <= SHORT, enough, general, results, (queries, keys, values, grads)
    )


def solution(mesh):
    return jax.shard_map(
        on_device,
        mesh=mesh,
        in_specs=(
            P(("ctx", "head"), None),
            P(("ctx", "head"), None),
            P(("ctx", "head"), None),
            P(("ctx", "head"), None),
            P(),
            P(),
            P(),
        ),
        out_specs=(P("ctx", "head"), P("ctx", "head"), P("ctx", "head"), P("ctx", "head")),
        check_vma=False,
    )
```

```python
import functools

import jax
import jax.numpy as jnp
from jax import lax
from jax.experimental import pallas as pl
from jax.experimental.pallas import tpu as pltpu
from jax.sharding import PartitionSpec as P

HD = 128
BLOCK = 256
SPAN = 7
SHORT = 9
CTX = 32
HEADS = 8
GROUP = 4
ROWS = 64
PIECE = 16
MESH = pl.DeviceIdType.MESH
LOG2E = 1.4426950408889634
SCALE = HD**-0.5
AHEAD = 6
LAST = (((1,), (1,)), ((), ()))
FIRST = (((0,), (0,)), ((), ()))


def drain(ref, sem):
    pltpu.make_async_copy(ref, ref, sem).wait()


def loop(count, body):
    def step(index, carry):
        body(index)
        return carry

    lax.fori_loop(0, count, step, 0)


def grouped(count, ready, send):
    def several(first, size):
        for u in range(size):
            ready(first + u)
        for u in range(size):
            send(first + u)

    loop(count // 4, lambda index: several(index * 4, 4))
    several(count // 4 * 4, count % 4)


def greet(me, head):
    barrier = pltpu.get_barrier_semaphore()
    chip = lax.div(me, 2)

    def signal(ctx, z):
        pl.semaphore_signal(barrier, inc=1, device_id=(ctx, z), device_id_type=MESH)

    loop(CTX - 1, lambda r: signal(lax.rem(me + r + 1, CTX), head))
    loop(HEADS - 1, lambda r: signal(me, lax.rem(head + r + 1, HEADS)))
    for half in range(2):
        source = half * 4 + lax.div(chip, 4)
        loop(CTX - 1, lambda r: signal(lax.rem(me + r + 1, CTX), source))

        @pl.when(source != head)
        def _():
            signal(me, source)

    apart = lax.rem(lax.div(chip, 4) + 4 - lax.rem(head, 4), 4)
    pl.semaphore_wait(barrier, CTX - 1 + HEADS - 1 + 2 * CTX - 1 + lax.div(apart + 3, 4))


def fused_kernel(
    slots,
    docs,
    order_ref,
    inverse_ref,
    first_ref,
    lengths_ref,
    q_ref,
    k_ref,
    v_ref,
    g_ref,
    o_ref,
    dq_ref,
    dk_ref,
    dv_ref,
    most_ref,
    table,
    q_buf,
    g_buf,
    g_scaled,
    turned,
    o_turned,
    kv,
    pieces,
    staged,
    bias,
    scores,
    probs,
    grads,
    wide_keys,
    wide_values,
    maxima,
    totals,
    inverses,
    inverse_rows,
    delta,
    sums,
    part,
    o_buf,
    dq_buf,
    arrived,
    summed,
    landed,
    piece_send,
    piece_recv,
    wide_send,
    wide_recv,
    list_send,
    list_recv,
    out_sem,
    part_send,
    part_recv,
    sum_send,
    sum_recv,
):
    me = lax.axis_index("ctx")
    head = lax.axis_index("head")
    chip, kind = lax.div(me, 2), lax.rem(me, 2)
    greet(me, head)

    def remote(src, dst, send, recv, ctx, z):
        pltpu.make_async_remote_copy(
            src_ref=src,
            dst_ref=dst,
            send_sem=send,
            recv_sem=recv,
            device_id=(ctx, z),
            device_id_type=MESH,
        ).start()

    pair = lax.div(head, 4)

    def send_pieces(which):
        ref = (k_ref, v_ref)[which]
        slot = pieces.at[me * 2 + pair]

        def piece(p, z):
            rows = pl.ds(pl.multiple_of(p * PIECE, PIECE), PIECE)
            return ref.at[rows, pl.ds(pl.multiple_of(z * HD, HD), HD)]

        def target(p):
            return (lax.rem(head, 4) * 4 + p) * 2 + which

        def send_piece(r):
            p, z = lax.rem(r, 4), lax.rem(head + lax.div(r, 4) + 1, HEADS)
            remote(piece(p, z), slot, piece_send, piece_recv, target(p), z)

        loop(4 * (HEADS - 1), send_piece)
        for p in range(4):

            @pl.when(target(p) != me)
            def _(p=p):
                remote(piece(p, head), slot, piece_send, piece_recv, target(p), head)

            @pl.when(target(p) == me)
            def _(p=p):
                pltpu.make_async_copy(piece(p, head), slot, piece_recv).start()

    send_pieces(0)
    send_pieces(1)

    my_rows = pl.ds(pl.multiple_of(lax.rem(head, 4) * ROWS, ROWS), ROWS)

    def columns(z, g):
        return pl.ds(pl.multiple_of(z * GROUP * HD + g * HD, HD), HD)

    def send_chunk(chunk):
        which, g = divmod(chunk, GROUP)
        ref, buf = ((q_ref, q_buf), (g_ref, g_buf))[which]

        def send_wide(r):
            z = lax.rem(head + r + 1, HEADS)
            remote(
                ref.at[:, columns(z, g)],
                buf.at[g, pair, my_rows],
                wide_send.at[which],
                wide_recv.at[which, g],
                me,
                z,
            )

        loop(HEADS - 1, send_wide)
        pltpu.make_async_copy(
            ref.at[:, columns(head, g)], buf.at[g, pair, my_rows], wide_recv.at[which, g]
        ).start()

    def take_chunk(chunk):
        which, g = divmod(chunk, GROUP)
        drain((q_buf, g_buf)[which].at[g], wide_recv.at[which, g])
        if chunk + AHEAD < 2 * GROUP:
            send_chunk(chunk + AHEAD)

    for chunk in range(AHEAD):
        send_chunk(chunk)

    rows = lax.broadcasted_iota(jnp.int32, (BLOCK, BLOCK), 0)
    cols = lax.broadcasted_iota(jnp.int32, (BLOCK, BLOCK), 1)

    def pair_of(device):
        block_a, block_b = order_ref[2 * device], order_ref[2 * device + 1]
        return block_a, block_b, block_a - first_ref[block_a] + 1

    block_a, block_b, count_a = pair_of(me)
    count_b = block_b - first_ref[block_b] + 1

    def belongs(t):
        return (t == 1) | (t > count_a)

    def chosen(t):
        return belongs(t).astype(jnp.int32)

    def make_bias(t):
        late = belongs(t)
        block = jnp.where(late, block_b, block_a)
        back = jnp.where(t < 2, 0, jnp.where(late, t - count_a, t - 1))
        reach = jnp.where(t < count_a + count_b, back * BLOCK, -2 * BLOCK)
        low = jnp.zeros((BLOCK, BLOCK), jnp.int32)
        end = 0
        for doc in range(docs - 1):
            end = end + lengths_ref[doc]
            low = jnp.where(cols + block * BLOCK >= end, end, low)
        allowed = (rows + (block - back) * BLOCK >= low) & (rows - cols <= reach)
        bias[t] = jnp.where(allowed, 0.0, -jnp.inf)

    def rows_of(device):
        return pl.ds(pl.multiple_of(lax.div(device, 2) * PIECE, PIECE), PIECE)

    def send_lists():
        def stage(peer):
            first_block, second_block, first_count = pair_of(peer)
            for slot in range(slots):
                if slot < 2:
                    wanted = (first_block, second_block)[slot]
                else:
                    wanted = jnp.where(
                        slot <= first_count,
                        first_block - slot + 1,
                        second_block - slot + first_count,
                    )
                staged[peer, slot] = pieces[inverse_ref[jnp.maximum(wanted, 0)]]

        def send_list(r):
            peer = lax.rem(me + r + 1, CTX)
            remote(
                staged.at[peer],
                kv.at[kind, :, rows_of(me)],
                list_send,
                list_recv.at[kind],
                peer,
                head,
            )

        grouped(CTX - 1, lambda r: stage(lax.rem(me + r + 1, CTX)), send_list)
        stage(me)
        pltpu.make_async_copy(
            staged.at[me], kv.at[kind, :, rows_of(me)], list_recv.at[kind]
        ).start()

    def first_round():
        drain(pieces, piece_recv)
        send_lists()

    pl.when(kind == 0)(first_round)
    take_chunk(0)
    loop(slots, make_bias)
    take_chunk(1)

    def tile_count(device, most):
        first_block, second_block, first_count = pair_of(device)
        return jnp.maximum(most, first_count + second_block - first_ref[second_block] + 1)

    most_ref[0] = lax.fori_loop(0, CTX, tile_count, 0)
    take_chunk(2)
    def second_round():
        drain(pieces, piece_recv)
        send_lists()

    pl.when(kind == 1)(second_round)
    drain(kv.at[0], list_recv.at[0])

    zeros = jnp.zeros((HD, BLOCK), jnp.bfloat16)

    def widen(wide, which, t):
        turned = kv[which, t].T
        for i, flag in enumerate((~belongs(t), belongs(t))):
            wide[i * HD : (i + 1) * HD, tile_cols(t)] = jnp.where(flag, turned, zeros)

    def tiles(body, first=0, last=slots):
        unroll = last - first if slots == SHORT else 2

        def several(index):
            for u in range(unroll):
                body(first + index * unroll + u)

        loop((last - first) // unroll, several)

    def tile_cols(t):
        return pl.ds(pl.multiple_of(t * BLOCK, BLOCK), BLOCK)

    def fold(tile, combine):
        height = tile.shape[0]
        while height > 8:
            height //= 2
            tile = combine(tile[:height], tile[height:])
        return tile

    def send_out(buf, ref, g, which):
        for i in range(2):
            pltpu.make_async_copy(
                buf.at[g, i],
                ref.at[pl.ds(i * BLOCK, BLOCK), pl.ds(pl.multiple_of(g * HD, HD), HD)],
                out_sem.at[which],
            ).start()

    def forward(g):
        for i in range(2):
            turned[i] = q_buf[g, i].T
        maxima[...] = jnp.full_like(maxima, -jnp.inf)
        totals[...] = jnp.zeros_like(totals)

        def score(t):
            tile = jnp.dot(kv[0, t], turned[chosen(t)], preferred_element_type=jnp.float32)
            tile = tile + bias[t]
            scores[t] = tile
            top = fold(tile, jnp.maximum)
            for i in range(2):
                penalty = jnp.where(chosen(t) == i, 0.0, -jnp.inf)
                maxima[i] = jnp.maximum(maxima[i], top + penalty)

        tiles(score)
        for i in range(2):
            top = jnp.max(maxima[i], axis=0, keepdims=True) * (SCALE * LOG2E)
            maxima[i] = jnp.broadcast_to(top, (8, BLOCK))

        def weigh(t):
            tile = jnp.exp2(scores[t] * (SCALE * LOG2E) - maxima[chosen(t), :1])
            probs[g, tile_cols(t)] = tile.astype(jnp.bfloat16)
            part_sum = fold(tile, jnp.add)
            late = belongs(t).astype(jnp.float32)
            for i, flag in enumerate((1.0 - late, late)):
                totals[i] = totals[i] + part_sum * flag

        tiles(weigh)
        for i in range(2):
            inverse = 1.0 / jnp.sum(totals[i], axis=0, keepdims=True)
            inverses[g, i] = jnp.broadcast_to(inverse, (8, BLOCK))
            inverse_rows[g, i] = jnp.broadcast_to(inverse, (HD, BLOCK)).T

    def attend(g):
        both = jnp.dot(wide_values[...], probs[g], preferred_element_type=jnp.float32)
        for i in range(2):
            result = both[i * HD : (i + 1) * HD] * inverses[g, i, :1]
            o_turned[g, i] = result.astype(jnp.bfloat16)
            o_buf[g, i] = result.T.astype(jnp.bfloat16)
        send_out(o_buf, o_ref, g, 0)

    def prepare(g):
        for i in range(2):
            scaled = (g_buf[g, i].astype(jnp.float32) * inverse_rows[g, i]).astype(jnp.bfloat16)
            g_scaled[g, i] = scaled

    def turn(g):
        for i in range(2):
            turned[i] = g_scaled[g, i].T
            product = o_turned[g, i].astype(jnp.float32) * turned[i].astype(jnp.float32)
            total = jnp.sum(fold(product, jnp.add), axis=0, keepdims=True)
            delta[i] = jnp.broadcast_to(total, (8, BLOCK))

    def value_grad(g, store, *span):
        def step(t):
            store(
                t,
                jnp.dot(
                    probs[g, tile_cols(t)],
                    g_scaled[g, chosen(t)],
                    preferred_element_type=jnp.float32,
                ),
            )

        tiles(step, *span)

    def key_grad(g, store, *span):
        def step(t):
            prob_grad = jnp.dot(kv[1, t], turned[chosen(t)], preferred_element_type=jnp.float32)
            score_grad = (
                probs[g, tile_cols(t)].astype(jnp.float32)
                * (prob_grad - delta[chosen(t), :1])
            ).astype(jnp.bfloat16)
            grads[g, tile_cols(t)] = score_grad
            store(
                t, jnp.dot(score_grad, q_buf[g, chosen(t)], preferred_element_type=jnp.float32)
            )

        tiles(step, *span)

    def query_grad(g):
        both = jnp.dot(wide_keys[...], grads[g], preferred_element_type=jnp.float32)
        for i in range(2):
            dq_buf[g, i] = (both[i * HD : (i + 1) * HD] * SCALE).T.astype(jnp.bfloat16)
        send_out(dq_buf, dq_ref, g, 1)

    sums[...] = jnp.zeros_like(sums)
    others = slots - 2

    def keep(which):
        def store(t, value):
            sums[which, t] = sums[which, t] + value

        return store

    def finish(which, factor):
        def store(t, value):
            part[which, t] = ((sums[which, t] + value) * factor).astype(jnp.bfloat16)

        return store

    def send_parts(which):
        def send_part(peer_chip, core):
            peer = peer_chip * 2 + core
            remote(
                part.at[which, pl.ds(2, others), rows_of(peer)],
                arrived.at[pl.ds(me * others, others)],
                part_send,
                part_recv,
                peer,
                head,
            )

        loop(15, lambda r: send_part(lax.rem(chip + r + 1, 16), which))

        @pl.when(kind != which)
        def _():
            send_part(chip, which)

        @pl.when(kind == which)
        def _():
            pltpu.make_async_copy(
                part.at[which, pl.ds(2, others), rows_of(me)],
                arrived.at[pl.ds(me * others, others)],
                part_recv,
            ).start()

    loop(slots, functools.partial(widen, wide_keys, 0))
    for g in range(GROUP):
        if g >= 3:
            take_chunk(g)
        forward(g)
    for g in range(GROUP - 1):
        take_chunk(GROUP + g)
        prepare(g)
        value_grad(g, keep(1))
    drain(kv.at[1], list_recv.at[1])
    loop(slots, functools.partial(widen, wide_values, 1))
    loop(GROUP, attend)

    def early(g):
        turn(g)
        key_grad(g, keep(0))

    last = GROUP - 1
    take_chunk(GROUP + last)
    prepare(last)
    value_grad(last, finish(1, 1.0), 2, slots)
    send_parts(1)
    loop(last, early)
    turn(last)
    key_grad(last, finish(0, SCALE), 2, slots)
    send_parts(0)
    value_grad(last, finish(1, 1.0), 0, 2)
    key_grad(last, finish(0, SCALE), 0, 2)
    loop(GROUP, query_grad)

    nowhere = CTX * others

    def make_table(place):
        block = order_ref[place]
        for step in range(SPAN - 1):
            query = jnp.minimum(block + step + 1, 2 * CTX - 1)
            spot = inverse_ref[query]
            device = lax.div(spot, 2)
            ahead = jnp.where(lax.rem(spot, 2) == 1, pair_of(device)[2] - 1, 0)
            listed = (block + step + 1 == query) & (first_ref[query] <= block)
            spot = jnp.minimum(device * others + ahead + step, nowhere)
            table[place * SPAN + step] = jnp.where(listed, spot, nowhere)

    loop(2 * CTX, make_table)
    arrived[nowhere] = jnp.zeros(arrived.shape[1:], arrived.dtype)
    drain(arrived.at[pl.ds(0, nowhere)], part_recv)

    def add_up(peer):
        for block in range(2):
            first = (peer * 2 + block) * SPAN
            total = arrived[table[first]].astype(jnp.float32)
            for step in range(1, SPAN - 1):
                total = total + arrived[table[first + step]].astype(jnp.float32)
            summed[peer, block] = total.astype(summed.dtype)

    def send_sum(r):
        peer = lax.rem(me + r + 1, CTX)
        remote(
            summed.at[peer],
            landed.at[kind, :, rows_of(me)],
            sum_send,
            sum_recv.at[kind],
            peer,
            head,
        )

    grouped(CTX - 1, lambda r: add_up(lax.rem(me + r + 1, CTX)), send_sum)
    add_up(me)
    pltpu.make_async_copy(
        summed.at[me], landed.at[kind, :, rows_of(me)], sum_recv.at[kind]
    ).start()

    drain(pieces.at[pl.ds(0, ROWS - 1)], piece_send)

    @pl.when(lax.div(chip, 4) != lax.rem(head, 4))
    def _():
        drain(pieces.at[0], piece_send)

    for buf, which in ((q_buf, 0), (g_buf, 1)):
        for g in range(GROUP):
            drain(buf.at[g, 0], wide_send.at[which])
            drain(buf.at[g, 1, pl.ds(0, 3 * ROWS)], wide_send.at[which])
    drain(staged.at[pl.ds(0, CTX - 1)], list_send)
    drain(arrived.at[pl.ds(0, (CTX - 1) * others)], part_send)
    drain(summed.at[pl.ds(0, CTX - 1)], sum_send)
    drain(o_buf, out_sem.at[0])
    drain(dq_buf, out_sem.at[1])
    for which, out_ref in ((1, dv_ref), (0, dk_ref)):
        drain(landed.at[which], sum_recv.at[which])
        for i in range(2):
            total = landed[which, i].astype(jnp.float32) + part[which, i].astype(jnp.float32)
            out_ref[i] = total.astype(jnp.bfloat16)


def fused(slots, identity, scalars, queries, keys, values, grads):
    docs = scalars[-1].shape[0]
    anywhere = pl.BlockSpec(memory_space=pl.ANY)
    small = pl.BlockSpec(memory_space=pltpu.SMEM)
    bf16, f32 = jnp.bfloat16, jnp.float32
    rows, wide = ROWS * HEADS, GROUP * HD
    dma = pltpu.SemaphoreType.DMA
    return pl.pallas_call(
        functools.partial(fused_kernel, slots, docs),
        out_shape=(
            jax.ShapeDtypeStruct((rows, wide), bf16),
            jax.ShapeDtypeStruct((rows, wide), bf16),
            jax.ShapeDtypeStruct((2, BLOCK, HD), bf16),
            jax.ShapeDtypeStruct((2, BLOCK, HD), bf16),
            jax.ShapeDtypeStruct((1,), jnp.int32),
        ),
        in_specs=[small] * 4 + [anywhere] * 4,
        out_specs=[anywhere] * 2 + [pl.BlockSpec(memory_space=pltpu.VMEM)] * 2 + [small],
        scratch_shapes=[
            pltpu.SMEM((2 * CTX * SPAN,), jnp.int32),
            pltpu.VMEM((GROUP, 2, BLOCK, HD), bf16),
            pltpu.VMEM((GROUP, 2, BLOCK, HD), bf16),
            pltpu.VMEM((GROUP, 2, BLOCK, HD), bf16),
            pltpu.VMEM((2, HD, BLOCK), bf16),
            pltpu.VMEM((GROUP, 2, HD, BLOCK), bf16),
            pltpu.VMEM((2, slots, BLOCK, HD), bf16),
            pltpu.VMEM((2 * CTX, PIECE, HD), bf16),
            pltpu.VMEM((CTX, slots, PIECE, HD), bf16),
            pltpu.VMEM((slots, BLOCK, BLOCK), f32),
            pltpu.VMEM((slots, BLOCK, BLOCK), f32),
            pltpu.VMEM((GROUP, slots * BLOCK, BLOCK), bf16),
            pltpu.VMEM((GROUP, slots * BLOCK, BLOCK), bf16),
            pltpu.VMEM((2 * HD, slots * BLOCK), bf16),
            pltpu.VMEM((2 * HD, slots * BLOCK), bf16),
            pltpu.VMEM((2, 8, BLOCK), f32),
            pltpu.VMEM((2, 8, BLOCK), f32),
            pltpu.VMEM((GROUP, 2, 8, BLOCK), f32),
            pltpu.VMEM((GROUP, 2, BLOCK, HD), f32),
            pltpu.VMEM((2, 8, BLOCK), f32),
            pltpu.VMEM((2, slots, BLOCK, HD), f32),
            pltpu.VMEM((2, slots, BLOCK, HD), bf16),
            pltpu.VMEM((GROUP, 2, BLOCK, HD), bf16),
            pltpu.VMEM((GROUP, 2, BLOCK, HD), bf16),
            pltpu.VMEM((CTX * (slots - 2) + 1, PIECE, HD), bf16),
            pltpu.VMEM((CTX, 2, PIECE, HD), bf16),
            pltpu.VMEM((2, 2, BLOCK, HD), bf16),
            dma,
            dma,
            dma((2,)),
            dma((2, GROUP)),
            dma,
            dma((2,)),
            dma((2,)),
            dma,
            dma,
            dma,
            dma((2,)),
        ],
        compiler_params=pltpu.CompilerParams(
            collective_id=identity, has_side_effects=True, vmem_limit_bytes=52 << 20
        ),
        name="fused",
    )(*scalars, queries, keys, values, grads)


def deliver_kernel(*refs):
    half = len(refs) // 2
    copies = [
        pltpu.make_async_copy(refs[i], refs[half + i], refs[2 * half].at[i]) for i in range(half)
    ]
    for copy in copies:
        copy.start()
    for copy in copies:
        copy.wait()


def deliver(*results):
    anywhere = pl.BlockSpec(memory_space=pl.ANY)
    return pl.pallas_call(
        deliver_kernel,
        out_shape=tuple(jax.ShapeDtypeStruct(r.shape, r.dtype) for r in results),
        in_specs=[anywhere] * len(results),
        out_specs=[anywhere] * len(results),
        scratch_shapes=[pltpu.SemaphoreType.DMA((len(results),))],
        name="deliver",
    )(*results)


def on_device(queries, keys, values, grads, lengths, key_first, order):
    ids = jnp.arange(2 * CTX, dtype=jnp.int32)
    inverse = jnp.sum(jnp.where(order[None, :] == ids[:, None], ids[None, :], 0), axis=1)
    scalars = (order, inverse, key_first, lengths)
    *results, most = fused(SHORT, 0, scalars, queries, keys, values, grads)

    def deliver_results(*results):
        rows = results[0].shape[0]
        return deliver(*(r.reshape(rows, r.shape[-1]) for r in results))

    def enough(results, arrays):
        return deliver_results(*results)

    def general(results, arrays):
        return deliver_results(*fused(2 * SPAN, 1, scalars, *arrays)[:4])

    return lax.cond(
        most[0] <= SHORT, enough, general, results, (queries, keys, values, grads)
    )


def solution(mesh):
    return jax.shard_map(
        on_device,
        mesh=mesh,
        in_specs=(
            P(("ctx", "head"), None),
            P(("ctx", "head"), None),
            P(("ctx", "head"), None),
            P(("ctx", "head"), None),
            P(),
            P(),
            P(),
        ),
        out_specs=(P("ctx", "head"), P("ctx", "head"), P("ctx", "head"), P("ctx", "head")),
        check_vma=False,
    )
```
